256 devices in a mesh: seq: 16 (over y_lo, x, core), head: 16 (over z, y_hi).
Axes of the slice: x: 4, y: 4 (y_hi: 2, y_lo: 2; y = y_hi * 2 + y_lo), z: 8, core: 2. Of those that a mesh axis runs over, the one named last changes fastest.
Arguments:
- queries: bfloat16 [32768, 8192], P(('seq', 'head')), may hold values from -8 to 8
- keys: bfloat16 [32768, 1024], P(('seq', 'head')), may hold values from -4 to 4
- values: bfloat16 [32768, 1024], P(('seq', 'head')), may hold values from -6 to 6
- band_tiles: int32 [64], replicated, may hold values from 1 to 16, as said below
- vertical_tiles: int32 [64, 16], replicated, may hold values from 0 to 255, as said below
- head_order: int32 [64], replicated, may hold values from 0 to 63, as said below
Outputs:
- attention: bfloat16 [32768, 8192], P(('seq', 'head'))
The draws below stay inside these ranges and needn't reach their ends.
Inputs may be any that keep to these rules, and one draw needn't show every extreme that they name: band_tiles[h] is the width of head h's band in tiles. vertical_tiles[h, g] is a tile of sequence group g: between g * 16 and (g + 1) * 16 - 1. `head_order`: a permutation of the heads; positions d * 4 to (d + 1) * 4 - 1 are the heads that index d of head serves.
All inputs are finite; a program needn't handle non-finite values.
Results may differ from the reference program's by a relative error of at most 0.0049.
Values may be sent and summed in bfloat16 or wider, within the bound.
A program may use at most 128 MiB of HBM per device.

```python
import jax
import jax.numpy as jnp
from jax import lax

HEADS = 64
KV_HEADS = 8
HD = 128
TILE = 128
SLASH_MAX = 16
TOKENS = 32768
SLOTS = 4
GROUP_TILES = 16
WMAX = 16
N_SEQ = 16


def draw_keys(key, part):
    key = jax.random.fold_in(key, 3)
    drawn = jnp.clip(jax.random.normal(key, (TOKENS, KV_HEADS * HD), jnp.float32), -4.0, 4.0)
    return drawn.astype(jnp.bfloat16)


def draw_queries(key, part):
    key = jax.random.fold_in(key, 4)
    drawn = 2.0 * jnp.clip(jax.random.normal(key, (TOKENS, HEADS * HD), jnp.float32), -4.0, 4.0)
    return drawn.astype(jnp.bfloat16)


def band_draw(key):
    key = jax.random.fold_in(key, 21)
    key_spread, key_widest, key_narrow, key_order = jax.random.split(key, 4)
    spread = jax.random.randint(key_spread, (HEADS,), 0, WMAX)
    widths = 1 + spread * spread // WMAX
    widest_head = jax.random.randint(key_widest, (), 0, HEADS)
    narrow_head = (widest_head + 1 + jax.random.randint(key_narrow, (), 0, HEADS - 1)) % HEADS
    head_ids = jnp.arange(HEADS, dtype=jnp.int32)
    widths = jnp.where(head_ids == widest_head, WMAX, widths)
    widths = jnp.where(head_ids == narrow_head, 1, widths)
    return (widths.astype(jnp.int32), key_order)


def draw_band_tiles(key, part):
    widths, key_order = band_draw(key)
    return widths


def draw_head_order(key, part):
    widths, key_order = band_draw(key)
    ranking = jax.random.permutation(key_order, HEADS).astype(jnp.int32)
    ordering = jnp.argsort(-(widths * HEADS + ranking), stable=True).astype(jnp.int32)
    device_count = HEADS // SLOTS
    places = jnp.arange(HEADS, dtype=jnp.int32)
    lap_index = places // device_count
    column = places % device_count
    device = jnp.where(lap_index % 2 == 0, column, device_count - 1 - column)
    target = device * SLOTS + lap_index
    return jnp.zeros((HEADS,), jnp.int32).at[target].set(ordering)


def draw_vertical_tiles(key, part):
    key = jax.random.fold_in(key, 5)
    key_inner, key_low, key_high = jax.random.split(key, 3)
    group_count = TOKENS // (GROUP_TILES * TILE)
    inner = jax.random.randint(key_inner, (HEADS, group_count), 0, GROUP_TILES)
    low_head = jax.random.randint(key_low, (), 0, HEADS)
    high_head = jax.random.randint(key_high, (), 0, HEADS)
    head_ids = jnp.arange(HEADS, dtype=jnp.int32)[:, None]
    group_ids = jnp.arange(group_count, dtype=jnp.int32)[None, :]
    inner = jnp.where((head_ids == low_head) & (group_ids == 0), 0, inner)
    inner = jnp.where((head_ids == high_head) & (group_ids == group_count - 1), GROUP_TILES - 1, inner)
    return (inner + group_ids * GROUP_TILES).astype(jnp.int32)


def level_of(key, shape, shards, low, high):
    def one(axis_at, blocks):
        draws = jax.random.uniform(jax.random.fold_in(jax.random.fold_in(key, 6), axis_at), (blocks,), jnp.float32, low / len(shards), high / len(shards))
        return jnp.repeat(jnp.exp(draws), shape[axis_at] // blocks).reshape((-1,) + (1,) * (len(shape) - axis_at - 1))

    gain = one(*shards[0])
    for cut in shards[1:]:
        gain = gain * one(*cut)
    return gain


def bell_draw(stream_key, extent, deviation, bound, pieces=(), kind=jnp.bfloat16):
    values = deviation * jax.random.normal(stream_key, extent, jnp.float32)
    if pieces:
        values = values * level_of(stream_key, extent, pieces, -0.22, 0.18)
    return jnp.clip(values, -bound, bound).astype(kind)


def setup_inputs(seed: int = 0) -> dict:
    splits = jax.random.split(jax.random.key(seed), 7)
    queries = draw_queries(jax.random.fold_in(splits[6], 71), 0)
    keys = draw_keys(jax.random.fold_in(splits[6], 71), 0)
    values = bell_draw(splits[2], (TOKENS, KV_HEADS * HD), 1.0, 6.0, ((0, 256),))
    band_tiles = draw_band_tiles(jax.random.fold_in(splits[6], 71), 0)
    vertical_tiles = draw_vertical_tiles(jax.random.fold_in(splits[6], 71), 0)
    head_order = draw_head_order(jax.random.fold_in(splits[6], 71), 0)
    return {"queries": queries, "keys": keys, "values": values, "band_tiles": band_tiles, "vertical_tiles": vertical_tiles, "head_order": head_order}


NEGATIVE = -1.0e30


def reference(queries, keys, values, band_tiles, vertical_tiles, head_order):
    row_count = queries.shape[0]
    tile_count = row_count // TILE
    group_tiles = tile_count // N_SEQ
    widest = min(SLASH_MAX, group_tiles)
    factor = HD ** -0.5
    heads_per_kv = HEADS // KV_HEADS
    tile_ids = jnp.arange(tile_count, dtype=jnp.int32)
    row_tiles = jnp.arange(row_count, dtype=jnp.int32) // TILE
    inside = jnp.arange(TILE)[:, None] >= jnp.arange(TILE)[None, :]

    def one_head(head_id):
        kv_head = head_id // heads_per_kv
        query_half = lax.dynamic_slice_in_dim(queries, head_id * HD, HD, 1)
        key_half = lax.dynamic_slice_in_dim(keys, kv_head * HD, HD, 1)
        value_half = lax.dynamic_slice_in_dim(values, kv_head * HD, HD, 1)
        query_tiles = query_half.astype(jnp.float32).reshape(tile_count, TILE, HD)
        zero_rows = jnp.zeros(((widest - 1) * TILE, HD), jnp.float32)
        key_padded = jnp.concatenate([zero_rows, key_half.astype(jnp.float32)], axis=0)
        value_padded = jnp.concatenate([zero_rows, value_half.astype(jnp.float32)], axis=0)
        band_width = band_tiles[head_id]

        def band_scores(offset):
            first_row = (widest - 1 - offset) * TILE
            key_tiles = lax.dynamic_slice_in_dim(key_padded, first_row, row_count, 0).reshape(tile_count, TILE, HD)
            scores = jnp.einsum("tqd,tkd->tqk", query_tiles, key_tiles) * factor
            usable = ((tile_ids - offset) >= 0)[:, None, None] & ((offset > 0) | inside)[None]
            return scores, usable

        chosen = vertical_tiles[head_id]
        far_keys = key_half.reshape(tile_count, TILE, HD)[chosen].reshape(N_SEQ * TILE, HD)
        far_values = value_half.reshape(tile_count, TILE, HD)[chosen].reshape(N_SEQ * TILE, HD)
        far_tile = jnp.repeat(chosen, TILE)
        far_scores = jnp.dot(query_half, far_keys.T, preferred_element_type=jnp.float32) * factor
        far_usable = far_tile[None, :] <= (row_tiles - band_width)[:, None]
        row_max = jnp.max(jnp.where(far_usable, far_scores, NEGATIVE), axis=1).reshape(tile_count, TILE)

        def raise_max(offset, current):
            scores, usable = band_scores(offset)
            return jnp.maximum(current, jnp.max(jnp.where(usable, scores, NEGATIVE), axis=2))

        row_max = lax.fori_loop(0, band_width, raise_max, row_max)
        flat_max = row_max.reshape(row_count)
        far_weight = jnp.where(far_usable, jnp.exp(far_scores - flat_max[:, None]), 0.0)
        row_mass = jnp.sum(far_weight, axis=1).reshape(tile_count, TILE)
        weighted = jnp.dot(far_weight.astype(jnp.bfloat16), far_values, preferred_element_type=jnp.float32)
        weighted = weighted.reshape(tile_count, TILE, HD)

        def add_band(offset, state_pair):
            mass_now, sum_now = state_pair
            scores, usable = band_scores(offset)
            weight = jnp.where(usable, jnp.exp(scores - row_max[..., None]), 0.0)
            rounded = lax.optimization_barrier(weight.astype(jnp.bfloat16)).astype(jnp.float32)
            first_row = (widest - 1 - offset) * TILE
            value_tiles = lax.dynamic_slice_in_dim(value_padded, first_row, row_count, 0).reshape(tile_count, TILE, HD)
            return mass_now + jnp.sum(weight, axis=2), sum_now + jnp.einsum("tqk,tkd->tqd", rounded, value_tiles)

        row_mass, weighted = lax.fori_loop(0, band_width, add_band, (row_mass, weighted))
        return (weighted / row_mass[..., None]).reshape(row_count, HD).astype(jnp.bfloat16)

    head_outputs = lax.map(one_head, head_order)
    return jnp.transpose(head_outputs, (1, 0, 2)).reshape(row_count, HEADS * HD)
```

```python
import functools

import jax
import jax.numpy as jnp
from jax import lax
from jax.experimental import pallas as pl
from jax.experimental.pallas import tpu as pltpu
from jax.sharding import PartitionSpec as P

HEADS = 64
HD = 128
TILE = 128
MESH = pl.DeviceIdType.MESH
NEG = -1e30
SCALE = 1.4426950408889634 * HD**-0.5
PLUS, MINUS = 0, 1
ARRIVALS = [(d, h) for h in range(1, 5) for d in (PLUS, MINUS)]


def device_id(ylo, x, yhi, z, c):
    return (ylo * 8 + x * 2 + c, z * 2 + yhi)


def kernel(
    band_ref,
    vert_ref,
    order_ref,
    q_ref,
    k_ref,
    v_ref,
    out_ref,
    kvs,
    kv,
    qb,
    far,
    vsel,
    ob,
    orecv,
    sb,
    mx,
    acc,
    den,
    q_ss,
    q_rs,
    a_ss,
    a_rs,
    z_ss,
    z_rs,
    b_ss,
    b_rs,
    f_ss,
    f_rs,
    o_ss,
    o_rs,
    t_s,
    y_s,

):
    seq, jj = lax.axis_index("seq"), lax.axis_index("head")
    ylo, x, c = seq // 8, (seq // 2) % 4, seq % 2
    z, yhi = jj // 2, jj % 2
    me = (x * 2 + yhi) * 2 + c
    kvh = x * 2 + yhi
    my_tile = (x * 2 + c) * 2 + yhi

    def member(o):
        return device_id(ylo, o // 4, (o // 2) % 2, z, o % 2)

    def tile_of(o):
        return ((o // 4) * 2 + o % 2) * 2 + (o // 2) % 2

    up = device_id(ylo, x, yhi, (z + 1) % 8, c)
    down = device_id(ylo, x, yhi, (z + 7) % 8, c)
    twin = device_id(ylo, x, yhi, z, 1 - c)
    across = device_id(1 - ylo, x, yhi, z, c)

    def send(src, dst, ss, rs, dev):
        return pltpu.make_async_remote_copy(
            src_ref=src, dst_ref=dst, send_sem=ss, recv_sem=rs, device_id=dev, device_id_type=MESH
        )

    barrier = pltpu.get_barrier_semaphore()
    for r in range(1, 16):
        pl.semaphore_signal(barrier, inc=1, device_id=member((me + r) % 16), device_id_type=MESH)
    for dev in (up, down, across):
        pl.semaphore_signal(barrier, inc=1, device_id=dev, device_id_type=MESH)

    for g in range(8):
        kvs[g, 0] = k_ref[:, g * HD : (g + 1) * HD]
        kvs[g, 1] = v_ref[:, g * HD : (g + 1) * HD]

    @pl.when(ylo == 0)
    def _():
        kv[0:16] = jnp.zeros((16, 2, TILE, HD), jnp.bfloat16)

    pl.semaphore_wait(barrier, 18)

    here = 16 + (x * 2 + c) * 16 + jj
    for r in range(1, 8):
        g = (kvh + r) % 8
        send(kvs.at[g], kv.at[here], a_ss.at[r], a_rs.at[r], member(g * 2 + c)).start()
    for r in range(1, 16):
        o = (me + r) % 16
        send(
            q_ref.at[:, pl.ds(pl.multiple_of(o * 512, 512), 512)],
            qb.at[my_tile],
            q_ss.at[r],
            q_rs.at[r],
            member(o),
        ).start()
    kv[here] = kvs[kvh]
    qb[my_tile] = q_ref[:, pl.ds(pl.multiple_of(me * 512, 512), 512)]
    for r in range(1, 8):
        g = (kvh + 8 - r) % 8
        at = 16 + ((g // 2) * 2 + c) * 16 + 2 * z + g % 2
        send(kvs.at[0], kv.at[at], a_ss.at[r], a_rs.at[r], twin).wait_recv()

    extra = (ylo == 1) & (c == 1)

    def block(nb, zz):
        first = 2 * zz if nb == 4 else 16 + (nb * 2 + c) * 16 + 2 * zz
        return kv.at[pl.ds(first, 2)]

    def twin_block(nb, zz):
        first = 2 * zz if nb == 4 else 16 + (nb * 2 + 1 - c) * 16 + 2 * zz
        return kv.at[pl.ds(first, 2)]

    def travels(d, h, nb):
        return h < 4 or (d == PLUS) == (nb in (0, 1, 4))

    def origin(d, h):
        return (z + 8 - h) % 8 if d == PLUS else (z + h) % 8

    def ring(d, h, nb):
        blk = block(nb, origin(d, h - 1))
        return send(blk, blk, z_ss.at[d, h - 1, nb], z_rs.at[d, h - 1, nb], up if d == PLUS else down)

    def ring_landing(d, h, nb):
        blk = block(nb, origin(d, h))
        return send(blk, blk, z_ss.at[d, h - 1, nb], z_rs.at[d, h - 1, nb], up if d == PLUS else down)

    def hand(q, nb, zz):
        blk = block(nb, zz)
        return send(blk, blk, b_ss.at[q, nb], b_rs.at[q, nb], twin)

    def handed(q, nb, zz):
        blk = twin_block(nb, zz)
        return send(blk, blk, b_ss.at[q, nb], b_rs.at[q, nb], twin)

    tail_src = kv.at[pl.ds(128 + 2 * z, 2)]
    tail_dst = kv.at[pl.ds(2 * z, 2)]
    tail = send(tail_src, tail_dst, t_s.at[0], t_s.at[1], across)

    @pl.when((ylo == 0) & (c == 1))
    def _():
        tail.start()

    def begin(nb):
        ring(PLUS, 1, nb).start()
        ring(MINUS, 1, nb).start()
        hand(0, nb, z).start()

    for nb in range(4):
        begin(nb)

    @pl.when(extra)
    def _():
        tail.wait_recv()
        begin(4)

    def arrive(q, d, h, nb):
        ring_landing(d, h, nb).wait_recv()
        if h < 4 and travels(d, h + 1, nb):
            ring(d, h + 1, nb).start()
        hand(q + 1, nb, origin(d, h)).start()

    for q, (d, h) in enumerate(ARRIVALS):
        for nb in range(4):
            if travels(d, h, nb):
                arrive(q, d, h, nb)
        if travels(d, h, 4):

            @pl.when(extra)
            def _():
                arrive(q, d, h, 4)

    def each_handed(act):
        for nb in range(5):

            def one():
                act(0, nb, z)
                for q, (d, h) in enumerate(ARRIVALS):
                    if travels(d, h, nb):
                        act(q + 1, nb, origin(d, h))

            yield nb, one

    for nb, one in each_handed(lambda q, nb, zz: handed(q, nb, zz).wait_recv()):
        if nb < 4:
            one()
        else:
            pl.when((ylo == 1) & (c == 0))(one)

    to_upper = send(vsel, far.at[z], y_s.at[0], y_s.at[1], across)

    def far_ring(d, h):
        blk = far.at[origin(d, h - 1)]
        return send(blk, blk, f_ss.at[d, h - 1], f_rs.at[d, h - 1], up if d == PLUS else down)

    def far_landing(d, h):
        blk = far.at[origin(d, h)]
        return send(blk, blk, f_ss.at[d, h - 1], f_rs.at[d, h - 1], up if d == PLUS else down)

    @pl.when(ylo == 0)
    def _():
        for a in range(4):
            vsel[a] = kv[16 + z * 16 + (vert_ref[me * 4 + a, z] & 15)]
        to_upper.start()
        to_upper.wait_send()

    far_hops = [(d, h) for d, h in ARRIVALS if not (d == MINUS and h == 4)]

    @pl.when(ylo == 1)
    def _():
        to_upper.wait_recv()
        far_ring(PLUS, 1).start()
        far_ring(MINUS, 1).start()
        for d, h in far_hops:
            far_landing(d, h).wait_recv()
            if (d, h + 1) in far_hops:
                far_ring(d, h + 1).start()

    def own_far(n, carry):
        g = ylo * 8 + n // 4
        a = n % 4
        far[g, a] = kv[16 + (n // 4) * 16 + (vert_ref[me * 4 + a, g] & 15)]
        return carry

    lax.fori_loop(0, 32, own_far, 0)

    for r in range(1, 16):
        o = (me + 16 - r) % 16
        send(
            q_ref.at[:, pl.ds(0, 512)], qb.at[tile_of(o)], q_ss.at[r], q_rs.at[r], member(o)
        ).wait_recv()

    rows_id = lax.broadcasted_iota(jnp.int32, (TILE, TILE), 0)
    cols_id = lax.broadcasted_iota(jnp.int32, (TILE, TILE), 1)

    def attend(mi, carry):
        gl, yh = mi // 2, mi % 2
        j = 2 * z + yh
        group = ylo * 8 + gl
        t = group * 16 + j
        start = gl * 16 + j + 1
        qs = [qb[mi, :, a * HD : (a + 1) * HD] for a in range(4)]
        q4 = jnp.concatenate(qs, axis=0)
        lims = [jnp.minimum(band_ref[me * 4 + a], t + 1) for a in range(4)]
        chunks = group // 4 + 1

        for cc in range(4):
            keys = kv[pl.ds(start + 4 * cc, 4), 0].reshape(512, HD)
            s = lax.dot_general(q4, keys, (((1,), (1,)), ((), ())), preferred_element_type=jnp.float32)
            for a in range(4):
                for i in range(4):
                    off = 15 - (4 * cc + i)
                    part = s[a * TILE : (a + 1) * TILE, i * TILE : (i + 1) * TILE]
                    if off == 0:
                        part = jnp.where(rows_id >= cols_id, part, NEG)
                    else:
                        part = part + jnp.where(off < lims[a], 0.0, NEG)
                    sb[cc, a * TILE : (a + 1) * TILE, i * TILE : (i + 1) * TILE] = part
                    if cc == 0 and i == 0:
                        mx[a * TILE : (a + 1) * TILE, :] = part
                    else:
                        mx[a * TILE : (a + 1) * TILE, :] = jnp.maximum(
                            mx[a * TILE : (a + 1) * TILE, :], part
                        )

        def far_scores(ch, carry):
            for a in range(4):
                keys = far[pl.ds(4 * ch, 4), a, 0].reshape(512, HD)
                s = lax.dot_general(
                    qs[a], keys, (((1,), (1,)), ((), ())), preferred_element_type=jnp.float32
                )
                for i in range(4):
                    ok = vert_ref[me * 4 + a, 4 * ch + i] <= t - band_ref[me * 4 + a]
                    part = s[:, i * TILE : (i + 1) * TILE] + jnp.where(ok, 0.0, NEG)
                    sb[4 + ch, a * TILE : (a + 1) * TILE, i * TILE : (i + 1) * TILE] = part
                    mx[a * TILE : (a + 1) * TILE, :] = jnp.maximum(
                        mx[a * TILE : (a + 1) * TILE, :], part
                    )
            return carry

        lax.fori_loop(0, chunks, far_scores, 0)

        top = jnp.max(mx[...], axis=1, keepdims=True) * SCALE
        mx[...] = jnp.broadcast_to(top, (512, HD))

        def weights(n, a):
            p = []
            m = mx[a * TILE : (a + 1) * TILE, :]
            total = None
            for i in range(4):
                w = jnp.exp2(sb[n, a * TILE : (a + 1) * TILE, i * TILE : (i + 1) * TILE] * SCALE - m)
                total = w if total is None else total + w
                p.append(w.astype(jnp.bfloat16))
            return jnp.concatenate(p, axis=1), total

        for cc in range(4):
            vals = kv[pl.ds(start + 4 * cc, 4), 1].reshape(512, HD)
            ps = []
            for a in range(4):
                p, total = weights(cc, a)
                ps.append(p)
                rows = slice(a * TILE, (a + 1) * TILE)
                den[rows, :] = total if cc == 0 else den[rows, :] + total
            pv = jnp.dot(jnp.concatenate(ps, axis=0), vals, preferred_element_type=jnp.float32)
            acc[...] = pv if cc == 0 else acc[...] + pv

        def far_values(ch, carry):
            for a in range(4):
                vals = far[pl.ds(4 * ch, 4), a, 1].reshape(512, HD)
                p, total = weights(4 + ch, a)
                rows = slice(a * TILE, (a + 1) * TILE)
                den[rows, :] = den[rows, :] + total
                acc[rows, :] = acc[rows, :] + jnp.dot(p, vals, preferred_element_type=jnp.float32)
            return carry

        lax.fori_loop(0, chunks, far_values, 0)
        res = acc[...] / jnp.sum(den[...], axis=1, keepdims=True)
        for a in range(4):
            ob[mi, a] = res[a * TILE : (a + 1) * TILE].astype(jnp.bfloat16)

        @pl.when(mi == my_tile)
        def _():
            orecv[pl.ds(me * 4, 4)] = ob[mi]

        @pl.when(mi != my_tile)
        def _():
            send(ob.at[mi], orecv.at[pl.ds(me * 4, 4)], o_ss.at[mi], o_rs.at[me], device_id(ylo, gl // 2, yh, z, gl % 2)).start()

        return carry

    lax.fori_loop(0, 16, attend, 0)

    for r in range(1, 16):
        o = (me + r) % 16
        send(ob.at[0], orecv.at[pl.ds(o * 4, 4)], o_ss.at[tile_of(o)], o_rs.at[o], member(o)).wait_recv()

    for p in range(HEADS):
        out_ref[:, p * HD : (p + 1) * HD] = orecv[order_ref[p]]

    for r in range(1, 8):
        send(kvs.at[0], kv.at[here], a_ss.at[r], a_rs.at[r], twin).wait_send()
    for r in range(1, 16):
        o = (me + r) % 16
        send(q_ref.at[:, pl.ds(0, 512)], qb.at[my_tile], q_ss.at[r], q_rs.at[r], twin).wait_send()
        send(ob.at[0], orecv.at[pl.ds(me * 4, 4)], o_ss.at[tile_of(o)], o_rs.at[me], twin).wait_send()

    @pl.when((ylo == 0) & (c == 1))
    def _():
        tail.wait_send()

    for nb, one in each_handed(lambda q, nb, zz: hand(q, nb, zz).wait_send()):
        if nb < 4:
            one()
        else:
            pl.when(extra)(one)

    def ring_sent(nb):
        for d, h in ARRIVALS:
            if travels(d, h, nb):
                ring(d, h, nb).wait_send()

    for nb in range(4):
        ring_sent(nb)
    pl.when(extra)(functools.partial(ring_sent, 4))

    @pl.when(ylo == 1)
    def _():
        for d, h in far_hops:
            far_ring(d, h).wait_send()


def body(queries, keys, values, band_tiles, vertical_tiles, head_order):
    dma = pltpu.SemaphoreType.DMA
    vm = pl.BlockSpec(memory_space=pltpu.VMEM)
    sm = pl.BlockSpec(memory_space=pltpu.SMEM)
    bf, f32 = jnp.bfloat16, jnp.float32
    return pl.pallas_call(
        kernel,
        out_shape=jax.ShapeDtypeStruct((TILE, HEADS * HD), bf),
        in_specs=[sm, sm, sm, vm, vm, vm],
        out_specs=vm,
        scratch_shapes=[
            pltpu.VMEM((8, 2, TILE, HD), bf),
            pltpu.VMEM((144, 2, TILE, HD), bf),
            pltpu.VMEM((16, TILE, 512), bf),
            pltpu.VMEM((16, 4, 2, TILE, HD), bf),
            pltpu.VMEM((4, 2, TILE, HD), bf),
            pltpu.VMEM((16, 4, TILE, HD), bf),
            pltpu.VMEM((HEADS, TILE, HD), bf),
            pltpu.VMEM((8, 512, 512), f32),
            pltpu.VMEM((512, HD), f32),
            pltpu.VMEM((512, HD), f32),
            pltpu.VMEM((512, HD), f32),
            dma((16,)),
            dma((16,)),
            dma((8,)),
            dma((8,)),
            dma((2, 4, 5)),
            dma((2, 4, 5)),
            dma((9, 5)),
            dma((9, 5)),
            dma((2, 4)),
            dma((2, 4)),
            dma((16,)),
            dma((16,)),
            dma((2,)),
            dma((2,)),

        ],
        compiler_params=pltpu.CompilerParams(
            collective_id=0, has_side_effects=True, vmem_limit_bytes=58 * 2**20
        ),
        name="attention",
    )(band_tiles, vertical_tiles, head_order, queries, keys, values)


def solution(mesh):
    tokens = P(("seq", "head"), None)
    return jax.shard_map(
        body,
        mesh=mesh,
        in_specs=(tokens, tokens, tokens, P(), P(), P()),
        out_specs=tokens,
        check_vma=False,
    )
```

```python
import functools

import jax
import jax.numpy as jnp
from jax import lax
from jax.experimental import pallas as pl
from jax.experimental.pallas import tpu as pltpu
from jax.sharding import PartitionSpec as P

HEADS = 64
HD = 128
TILE = 128
MESH = pl.DeviceIdType.MESH
NEG = -1e30
SCALE = 1.4426950408889634 * HD**-0.5
PLUS, MINUS = 0, 1
ARRIVALS = [(d, h) for h in range(1, 5) for d in (PLUS, MINUS)]


def device_id(ylo, x, yhi, z, c):
    return (ylo * 8 + x * 2 + c, z * 2 + yhi)


def kernel(
    band_ref,
    vert_ref,
    order_ref,
    q_ref,
    k_ref,
    v_ref,
    out_ref,
    kvs,
    kv,
    qb,
    far,
    ob,
    orecv,
    sb,
    mx,
    acc1,
    den1,
    top1,
    q_ss,
    q_rs,
    a_ss,
    a_rs,
    z_ss,
    z_rs,
    b_ss,
    b_rs,
    y_ss,
    y_rs,
    f_ss,
    f_rs,
    o_ss,
    o_rs,
    t_s,
):
    seq, jj = lax.axis_index("seq"), lax.axis_index("head")
    ylo, x, c = seq // 8, (seq // 2) % 4, seq % 2
    z, yhi = jj // 2, jj % 2
    me = (x * 2 + yhi) * 2 + c
    kvh = x * 2 + yhi
    my_tile = (x * 2 + c) * 2 + yhi
    lower, upper = ylo == 0, ylo == 1
    extra = upper & (c == 1)
    f32, bf = jnp.float32, jnp.bfloat16
    rows = [slice(a * TILE, (a + 1) * TILE) for a in range(4)]

    def member(o):
        return device_id(ylo, o // 4, (o // 2) % 2, z, o % 2)

    def tile_of(o):
        return ((o // 4) * 2 + o % 2) * 2 + (o // 2) % 2

    def holder(mi):
        return device_id(ylo, mi // 4, mi % 2, z, (mi // 2) % 2)

    up = device_id(ylo, x, yhi, (z + 1) % 8, c)
    down = device_id(ylo, x, yhi, (z + 7) % 8, c)
    twin = device_id(ylo, x, yhi, z, 1 - c)
    across = device_id(1 - ylo, x, yhi, z, c)
    way = (up, down)

    def send(src, dst, ss, rs, dev):
        return pltpu.make_async_remote_copy(
            src_ref=src, dst_ref=dst, send_sem=ss, recv_sem=rs, device_id=dev, device_id_type=MESH
        )

    barrier = pltpu.get_barrier_semaphore()
    for r in range(1, 16):
        pl.semaphore_signal(barrier, inc=1, device_id=member((me + r) % 16), device_id_type=MESH)
    for dev in (up, down, across):
        pl.semaphore_signal(barrier, inc=1, device_id=dev, device_id_type=MESH)

    for g in range(8):
        kvs[g, 0] = k_ref[:, g * HD : (g + 1) * HD]
        kvs[g, 1] = v_ref[:, g * HD : (g + 1) * HD]

    @pl.when(lower)
    def _():
        kv[0:16] = jnp.zeros((16, 2, TILE, HD), bf)

    far[pl.ds(ylo * 8, 8)] = jnp.zeros((8, 4, 2, TILE, HD), bf)
    pl.semaphore_wait(barrier, 18)

    here = 16 + (x * 2 + c) * 16 + jj
    for r in range(1, 8):
        g = (kvh + r) % 8
        send(kvs.at[g], kv.at[here], a_ss.at[r], a_rs.at[kvh], member(g * 2 + c)).start()
    kv[here] = kvs[kvh]

    def q_send(r):
        o = (me + r) % 16
        return send(
            q_ref.at[:, pl.ds(pl.multiple_of(o * 512, 512), 512)],
            qb.at[my_tile],
            q_ss.at[r],
            q_rs.at[my_tile],
            member(o),
        )

    for r in range(1, 16):
        q_send(r).start()
    qb[my_tile] = q_ref[:, pl.ds(pl.multiple_of(me * 512, 512), 512)]

    def kv_landed(n):
        for yh in range(2):
            g = n * 2 + yh

            @pl.when(kvh != g)
            def _():
                at = 16 + (n * 2 + c) * 16 + 2 * z + yh
                send(kvs.at[0], kv.at[at], a_ss.at[1], a_rs.at[g], twin).wait_recv()

    def first_of(n, core, zz):
        return jnp.where(n == 4, 2 * zz, 16 + (n * 2 + core) * 16 + 2 * zz)

    def block(n, zz):
        return kv.at[pl.ds(first_of(n, c, zz), 2)]

    def origin(d, h):
        return (z + 8 - h) % 8 if d == PLUS else (z + h) % 8

    def goes(d, h, n):
        last = (n < 2) | (n == 4)
        return (h < 4) | (last if d == PLUS else jnp.logical_not(last))

    def ring(d, h, n):
        blk = block(n, origin(d, h - 1))
        return send(blk, blk, z_ss.at[d, h - 1, n], z_rs.at[d, h - 1, n], way[d])

    def ring_landing(d, h, n):
        blk = block(n, origin(d, h))
        return send(blk, blk, z_ss.at[d, h - 1, n], z_rs.at[d, h - 1, n], way[d])

    def slot(d, h):
        return 1 + (h - 1) * 2 + d

    def hand(q, n, zz):
        blk = block(n, zz)
        return send(blk, blk, b_ss.at[q, n], b_rs.at[q, n], twin)

    def handed(q, n, zz):
        blk = kv.at[pl.ds(first_of(n, 1 - c, zz), 2)]
        return send(blk, blk, b_ss.at[q, n], b_rs.at[q, n], twin)

    def begin(n):
        ring(PLUS, 1, n).start()
        ring(MINUS, 1, n).start()
        hand(0, n, z).start()

    def hop(n, h):
        for d in (PLUS, MINUS):

            @pl.when(goes(d, h, n))
            def _():
                ring_landing(d, h, n).wait_recv()

                @pl.when((h < 4) & goes(d, h + 1, n))
                def _():
                    ring(d, jnp.minimum(h + 1, 4), n).start()

                hand(slot(d, h), n, origin(d, h)).start()

    def every(n, act):
        act(0, n, z)
        for d, h in ARRIVALS:
            pl.when(goes(d, h, n))(functools.partial(act, slot(d, h), n, origin(d, h)))

    tail_src = kv.at[pl.ds(128 + 2 * z, 2)]
    tail_dst = kv.at[pl.ds(2 * z, 2)]
    tail = send(tail_src, tail_dst, t_s.at[0], t_s.at[1], across)

    kv_landed(0)
    begin(0)
    kv_landed(3)

    @pl.when(lower & (c == 1))
    def _():
        tail.start()

    kv_landed(1)
    kv_landed(2)

    @pl.when(extra)
    def _():
        tail.wait_recv()
        begin(4)

    hop(0, 1)
    begin(1)
    hop(0, 2)
    pl.when(extra)(functools.partial(hop, 4, 1))
    hop(0, 3)
    hop(1, 1)
    pl.when(extra)(functools.partial(hop, 4, 2))
    begin(2)
    hop(0, 4)
    hop(1, 2)
    pl.when(extra)(functools.partial(hop, 4, 3))
    pl.when(extra)(functools.partial(hop, 4, 4))
    pl.when(upper & (c == 0))(
        functools.partial(every, 4, lambda q, n, zz: handed(q, n, zz).wait_recv())
    )

    def pick(n):
        def one(e, carry):
            g, a = 2 * n + e // 4, e % 4
            want = vert_ref[me * 4 + a, ylo * 8 + g] & 15
            got = kv[16 + g * 16]
            for r in range(1, 16):
                got = jnp.where(want == r, kv[16 + g * 16 + r], got)
            far[ylo * 8 + g, a] = got
            return carry

        lax.fori_loop(0, 8, one, 0)

    def to_upper(n):
        blk = far.at[2 * n + z % 2]
        return send(blk, blk, y_ss.at[n], y_rs.at[n], across)

    def share(n, d, odd):
        blk = far.at[2 * n + odd, pl.ds(2 * d, 2)]
        return send(blk, blk, f_ss.at[n, d], f_rs.at[n, d], way[d])

    rows_id = lax.broadcasted_iota(jnp.int32, (TILE, TILE), 0)
    cols_id = lax.broadcasted_iota(jnp.int32, (TILE, TILE), 1)
    ones = jnp.ones((512, HD), bf)

    def put_scores(cc, a, parts):
        m = None
        for i in range(4):
            sb[cc, rows[a], rows[i]] = parts[i]
            m = parts[i] if m is None else jnp.maximum(m, parts[i])
        mx[cc, rows[a], :] = m

    def far_scores(cc, first, t, qs):
        for a in range(4):
            keys = far[pl.ds(first, 4), a, 0].reshape(512, HD)
            s = lax.dot_general(qs[a], keys, (((1,), (1,)), ((), ())), preferred_element_type=f32)
            parts = []
            for i in range(4):
                ok = vert_ref[me * 4 + a, first + i] <= t - band_ref[me * 4 + a]
                parts.append(s[:, rows[i]] + jnp.where(ok, 0.0, NEG))
            put_scores(cc, a, parts)

    def row_top(n, a):
        m = mx[0, rows[a], :]
        for cc in range(1, n):
            m = jnp.maximum(m, mx[cc, rows[a], :])
        return jnp.max(m, axis=1, keepdims=True) * SCALE

    def weights(cc, a, top):
        return jnp.concatenate(
            [jnp.exp2(sb[cc, rows[a], rows[i]] * SCALE - top).astype(bf) for i in range(4)], axis=1
        )

    def far_sums(cc, first, a, top):
        vals = jnp.concatenate([far[pl.ds(first, 4), a, 1].reshape(512, HD), ones], axis=1)
        return jnp.dot(weights(cc, a, top), vals, preferred_element_type=f32)

    def send_out(mi):
        @pl.when(mi == my_tile)
        def _():
            orecv[pl.ds(me * 4, 4)] = ob[mi]

        @pl.when(mi != my_tile)
        def _():
            send(ob.at[mi], orecv.at[pl.ds(me * 4, 4)], o_ss.at[mi], o_rs.at[me], holder(mi)).start()

    def place(mi):
        gl = mi // 2
        j = 2 * z + mi % 2
        return (ylo * 8 + gl) * 16 + j, gl * 16 + j + 1

    def queries_of(mi):
        return [qb[mi, :, rows[a]] for a in range(4)]

    def attend(mi, carry):
        n, k = mi // 4, mi % 4

        @pl.when((k == 0) & (n < 3))
        def _():
            hop(n + 1, 3)

        @pl.when((k == 1) & (n < 2))
        def _():
            hop(n + 2, 1)

        @pl.when((k == 2) & (n < 3))
        def _():
            hop(n + 1, 4)

        @pl.when((k == 2) & (n < 1))
        def _():
            begin(n + 3)

        @pl.when((k == 3) & (n < 2))
        def _():
            hop(n + 2, 2)

        @pl.when(k == 0)
        def _():
            every(n, lambda q, m, zz: handed(q, m, zz).wait_recv())
            pick(n)

            @pl.when(lower)
            def _():
                to_upper(n).start()

        @pl.when((k == 3) & upper)
        def _():
            to_upper(n).wait_recv()
            share(n, PLUS, z % 2).start()
            share(n, MINUS, z % 2).start()

        @pl.when(mi != my_tile)
        def _():
            send(q_ref.at[:, pl.ds(0, 512)], qb.at[mi], q_ss.at[1], q_rs.at[mi], twin).wait_recv()

        t, start = place(mi)
        qs = queries_of(mi)
        q4 = jnp.concatenate(qs, axis=0)
        lims = [jnp.minimum(band_ref[me * 4 + a], t + 1) for a in range(4)]
        for cc in range(4):
            keys = kv[pl.ds(start + 4 * cc, 4), 0].reshape(512, HD)
            s = lax.dot_general(q4, keys, (((1,), (1,)), ((), ())), preferred_element_type=f32)
            for a in range(4):
                parts = []
                for i in range(4):
                    off = 15 - (4 * cc + i)
                    part = s[rows[a], rows[i]]
                    if off == 0:
                        part = jnp.where(rows_id >= cols_id, part, NEG)
                    else:
                        part = part + jnp.where(off < lims[a], 0.0, NEG)
                    parts.append(part)
                put_scores(cc, a, parts)
        for ch in range(2):
            far_scores(4 + ch, ylo * 8 + 4 * ch, t, qs)

        @pl.when(mi >= 0)
        def _():
            tops = [row_top(6, a) for a in range(4)]
            acc = [None] * 4
            for cc in range(4):
                vals = jnp.concatenate([kv[pl.ds(start + 4 * cc, 4), 1].reshape(512, HD), ones], axis=1)
                p = jnp.concatenate([weights(cc, a, tops[a]) for a in range(4)], axis=0)
                pv = jnp.dot(p, vals, preferred_element_type=f32)
                for a in range(4):
                    acc[a] = pv[rows[a]] if cc == 0 else acc[a] + pv[rows[a]]
            for ch in range(2):
                for a in range(4):
                    acc[a] = acc[a] + far_sums(4 + ch, ylo * 8 + 4 * ch, a, tops[a])
            for a in range(4):
                acc1[mi, rows[a], :] = acc[a][:, :HD]
                den1[mi, rows[a], :] = acc[a][:, HD:]
                top1[mi, rows[a], :] = jnp.broadcast_to(tops[a], (TILE, HD))

        @pl.when(lower)
        def _():
            for a in range(4):
                ob[mi, a] = (acc1[mi, rows[a], :] / den1[mi, rows[a], :]).astype(bf)
            send_out(mi)

        return carry

    lax.fori_loop(0, 16, attend, 0)

    def attend_lower_groups(mi, carry):
        t, _ = place(mi)
        qs = queries_of(mi)
        for ch in range(2):
            far_scores(ch, 4 * ch, t, qs)

        @pl.when(mi >= 0)
        def _():
            for a in range(4):
                old = top1[mi, rows[a], :]
                top = jnp.maximum(row_top(2, a), old)
                keep = jnp.exp2(old - top)
                pv = far_sums(0, 0, a, top) + far_sums(1, 4, a, top)
                num = acc1[mi, rows[a], :] * keep + pv[:, :HD]
                mass = den1[mi, rows[a], :] * keep + pv[:, HD:]
                ob[mi, a] = (num / mass).astype(bf)

        send_out(mi)
        return carry

    @pl.when(upper)
    def _():
        for n in range(4):
            for d in (PLUS, MINUS):
                share(n, d, 1 - z % 2).wait_recv()
        lax.fori_loop(0, 16, attend_lower_groups, 0)

    for r in range(1, 16):
        o = (me + r) % 16
        send(ob.at[0], orecv.at[pl.ds(o * 4, 4)], o_ss.at[tile_of(o)], o_rs.at[o], member(o)).wait_recv()

    for p in range(HEADS):
        out_ref[:, p * HD : (p + 1) * HD] = orecv[order_ref[p]]

    for r in range(1, 8):
        send(kvs.at[0], kv.at[here], a_ss.at[r], a_rs.at[0], twin).wait_send()
    for r in range(1, 16):
        o = (me + r) % 16
        q_send(r).wait_send()
        send(ob.at[0], orecv.at[pl.ds(me * 4, 4)], o_ss.at[tile_of(o)], o_rs.at[me], twin).wait_send()

    @pl.when(lower & (c == 1))
    def _():
        tail.wait_send()

    def sent(n):
        every(n, lambda q, m, zz: hand(q, m, zz).wait_send())
        for d, h in ARRIVALS:
            pl.when(goes(d, h, n))(lambda d=d, h=h: ring(d, h, n).wait_send())

    def sent_in_loop(n, carry):
        sent(n)

        @pl.when(lower)
        def _():
            to_upper(n).wait_send()

        @pl.when(upper)
        def _():
            share(n, PLUS, z % 2).wait_send()
            share(n, MINUS, z % 2).wait_send()

        return carry

    lax.fori_loop(0, 4, sent_in_loop, 0)
    pl.when(extra)(functools.partial(sent, 4))


def body(queries, keys, values, band_tiles, vertical_tiles, head_order):
    dma = pltpu.SemaphoreType.DMA
    vm = pl.BlockSpec(memory_space=pltpu.VMEM)
    sm = pl.BlockSpec(memory_space=pltpu.SMEM)
    bf, f32 = jnp.bfloat16, jnp.float32
    return pl.pallas_call(
        kernel,
        out_shape=jax.ShapeDtypeStruct((TILE, HEADS * HD), bf),
        in_specs=[sm, sm, sm, vm, vm, vm],
        out_specs=vm,
        scratch_shapes=[
            pltpu.VMEM((8, 2, TILE, HD), bf),
            pltpu.VMEM((144, 2, TILE, HD), bf),
            pltpu.VMEM((16, TILE, 512), bf),
            pltpu.VMEM((16, 4, 2, TILE, HD), bf),
            pltpu.VMEM((16, 4, TILE, HD), bf),
            pltpu.VMEM((HEADS, TILE, HD), bf),
            pltpu.VMEM((6, 512, 512), f32),
            pltpu.VMEM((6, 512, HD), f32),
            pltpu.VMEM((16, 512, HD), f32),
            pltpu.VMEM((16, 512, HD), f32),
            pltpu.VMEM((16, 512, HD), f32),
            dma((16,)),
            dma((16,)),
            dma((8,)),
            dma((8,)),
            dma((2, 4, 5)),
            dma((2, 4, 5)),
            dma((9, 5)),
            dma((9, 5)),
            dma((4,)),
            dma((4,)),
            dma((4, 2)),
            dma((4, 2)),
            dma((16,)),
            dma((16,)),
            dma((2,)),
        ],
        compiler_params=pltpu.CompilerParams(
            collective_id=0, has_side_effects=True, vmem_limit_bytes=60 * 2**20
        ),
        name="attention",
    )(band_tiles, vertical_tiles, head_order, queries, keys, values)


def solution(mesh):
    tokens = P(("seq", "head"), None)
    return jax.shard_map(
        body,
        mesh=mesh,
        in_specs=(tokens, tokens, tokens, P(), P(), P()),
        out_specs=tokens,
        check_vma=False,
    )
```

```python
import functools

import jax
import jax.numpy as jnp
from jax import lax
from jax.experimental import pallas as pl
from jax.experimental.pallas import tpu as pltpu
from jax.sharding import PartitionSpec as P

HEADS = 64
HD = 128
TILE = 128
MESH = pl.DeviceIdType.MESH
NEG = -1e30
SCALE = 1.4426950408889634 * HD**-0.5
PLUS, MINUS = 0, 1
ARRIVALS = [(d, h) for h in range(1, 5) for d in (PLUS, MINUS)]

CHIPS = [(1, 0), (3, 0), (0, 1), (2, 0), (1, 1), (3, 1), (2, 1)]
PEERS = [(dx, dy, dc) for dy, dc in ((1, 0), (1, 1), (0, 1), (0, 0)) for dx in (1, 3, 0, 2)]
PEERS.remove((0, 0, 0))


def device_id(ylo, x, yhi, z, c):
    return (ylo * 8 + x * 2 + c, z * 2 + yhi)


def kernel(
    band_ref,
    vert_ref,
    order_ref,
    q_ref,
    k_ref,
    v_ref,
    out_ref,
    kvs,
    kv,
    qb,
    far,
    ob,
    orecv,
    sb,
    mx,
    acc1,
    den1,
    top1,
    q_ss,
    q_rs,
    a_ss,
    a_rs,
    z_ss,
    z_rs,
    b_ss,
    b_rs,
    y_ss,
    y_rs,
    f_ss,
    f_rs,
    o_ss,
    o_rs,
    t_s,
):
    seq, jj = lax.axis_index("seq"), lax.axis_index("head")
    ylo, x, c = seq // 8, (seq // 2) % 4, seq % 2
    z, yhi = jj // 2, jj % 2
    me = (x * 2 + yhi) * 2 + c
    kvh = x * 2 + yhi
    my_tile = (x * 2 + c) * 2 + yhi
    lower, upper = ylo == 0, ylo == 1
    extra = upper & (c == 1)
    f32, bf = jnp.float32, jnp.bfloat16
    rows = [slice(a * TILE, (a + 1) * TILE) for a in range(4)]

    def member(o):
        return device_id(ylo, o // 4, (o // 2) % 2, z, o % 2)

    def tile_of(o):
        return ((o // 4) * 2 + o % 2) * 2 + (o // 2) % 2

    def holder(mi):
        return device_id(ylo, mi // 4, mi % 2, z, (mi // 2) % 2)

    up = device_id(ylo, x, yhi, (z + 1) % 8, c)
    down = device_id(ylo, x, yhi, (z + 7) % 8, c)
    twin = device_id(ylo, x, yhi, z, 1 - c)
    across = device_id(1 - ylo, x, yhi, z, c)
    way = (up, down)

    def send(src, dst, ss, rs, dev):
        return pltpu.make_async_remote_copy(
            src_ref=src, dst_ref=dst, send_sem=ss, recv_sem=rs, device_id=dev, device_id_type=MESH
        )

    barrier = pltpu.get_barrier_semaphore()
    for r in range(1, 16):
        pl.semaphore_signal(barrier, inc=1, device_id=member((me + r) % 16), device_id_type=MESH)
    for dev in (up, down, across):
        pl.semaphore_signal(barrier, inc=1, device_id=dev, device_id_type=MESH)

    for g in range(8):
        kvs[g, 0] = k_ref[:, g * HD : (g + 1) * HD]
        kvs[g, 1] = v_ref[:, g * HD : (g + 1) * HD]

    @pl.when(lower)
    def _():
        kv[0:16] = jnp.zeros((16, 2, TILE, HD), bf)

    far[pl.ds(ylo * 8, 8)] = jnp.zeros((8, 4, 2, TILE, HD), bf)
    pl.semaphore_wait(barrier, 18)

    here = 16 + (x * 2 + c) * 16 + jj
    for r, (dx, dy) in enumerate(CHIPS):
        g = ((x + dx) % 4) * 2 + (yhi + dy) % 2
        send(kvs.at[g], kv.at[here], a_ss.at[r], a_rs.at[kvh], member(g * 2 + c)).start()
    kv[here] = kvs[kvh]

    def q_send(r):
        dx, dy, dc = PEERS[r - 1]
        o = (((x + dx) % 4) * 2 + (yhi + dy) % 2) * 2 + (c + dc) % 2
        return send(
            q_ref.at[:, pl.ds(pl.multiple_of(o * 512, 512), 512)],
            qb.at[my_tile],
            q_ss.at[r],
            q_rs.at[my_tile],
            member(o),
        )

    qb[my_tile] = q_ref[:, pl.ds(pl.multiple_of(me * 512, 512), 512)]

    def kv_landed(n):
        for yh in range(2):
            g = n * 2 + yh

            @pl.when(kvh != g)
            def _():
                at = 16 + (n * 2 + c) * 16 + 2 * z + yh
                send(kvs.at[0], kv.at[at], a_ss.at[1], a_rs.at[g], twin).wait_recv()

    def first_of(n, core, zz):
        return jnp.where(n == 4, 2 * zz, 16 + (n * 2 + core) * 16 + 2 * zz)

    def block(n, zz):
        return kv.at[pl.ds(first_of(n, c, zz), 2)]

    def origin(d, h):
        return (z + 8 - h) % 8 if d == PLUS else (z + h) % 8

    def goes(d, h, n):
        last = (n < 2) | (n == 4)
        return (h < 4) | (last if d == PLUS else jnp.logical_not(last))

    def ring(d, h, n):
        blk = block(n, origin(d, h - 1))
        return send(blk, blk, z_ss.at[d, h - 1, n], z_rs.at[d, h - 1, n], way[d])

    def ring_landing(d, h, n):
        blk = block(n, origin(d, h))
        return send(blk, blk, z_ss.at[d, h - 1, n], z_rs.at[d, h - 1, n], way[d])

    def slot(d, h):
        return 1 + (h - 1) * 2 + d

    def hand(q, n, zz):
        blk = block(n, zz)
        return send(blk, blk, b_ss.at[q, n], b_rs.at[q, n], twin)

    def handed(q, n, zz):
        blk = kv.at[pl.ds(first_of(n, 1 - c, zz), 2)]
        return send(blk, blk, b_ss.at[q, n], b_rs.at[q, n], twin)

    def begin(n):
        ring(PLUS, 1, n).start()
        ring(MINUS, 1, n).start()
        hand(0, n, z).start()

    def hop(n, h):
        for d in (PLUS, MINUS):

            @pl.when(goes(d, h, n))
            def _():
                ring_landing(d, h, n).wait_recv()

                @pl.when((h < 4) & goes(d, h + 1, n))
                def _():
                    ring(d, jnp.minimum(h + 1, 4), n).start()

                hand(slot(d, h), n, origin(d, h)).start()

    def every(n, act):
        act(0, n, z)
        for d, h in ARRIVALS:
            pl.when(goes(d, h, n))(functools.partial(act, slot(d, h), n, origin(d, h)))

    tail_src = kv.at[pl.ds(128 + 2 * z, 2)]
    tail_dst = kv.at[pl.ds(2 * z, 2)]
    tail = send(tail_src, tail_dst, t_s.at[0], t_s.at[1], across)

    kv_landed(0)
    begin(0)
    for r in range(1, 16):
        q_send(r).start()
    kv_landed(1)
    begin(1)
    hop(0, 1)
    kv_landed(2)
    begin(2)
    hop(0, 2)
    hop(1, 1)
    kv_landed(3)
    begin(3)

    @pl.when(lower & (c == 1))
    def _():
        tail.start()

    hop(0, 3)
    hop(1, 2)
    hop(2, 1)
    hop(0, 4)
    hop(1, 3)
    hop(2, 2)
    hop(3, 1)

    def pick(n):
        def one(e, carry):
            g, a = 2 * n + e // 4, e % 4
            want = vert_ref[me * 4 + a, ylo * 8 + g] & 15
            got = kv[16 + g * 16]
            for r in range(1, 16):
                got = jnp.where(want == r, kv[16 + g * 16 + r], got)
            far[ylo * 8 + g, a] = got
            return carry

        lax.fori_loop(0, 8, one, 0)

    def to_upper(n):
        blk = far.at[2 * n + z % 2]
        return send(blk, blk, y_ss.at[n], y_rs.at[n], across)

    def share(n, d, odd):
        blk = far.at[2 * n + odd, pl.ds(2 * d, 2)]
        return send(blk, blk, f_ss.at[n, d], f_rs.at[n, d], way[d])

    rows_id = lax.broadcasted_iota(jnp.int32, (TILE, TILE), 0)
    cols_id = lax.broadcasted_iota(jnp.int32, (TILE, TILE), 1)
    ones = jnp.ones((512, HD), bf)

    def put_scores(cc, a, parts):
        m = None
        for i in range(4):
            sb[cc, rows[a], rows[i]] = parts[i]
            m = parts[i] if m is None else jnp.maximum(m, parts[i])
        mx[cc, rows[a], :] = m

    def far_scores(cc, first, t, qs):
        for a in range(4):
            keys = far[pl.ds(first, 4), a, 0].reshape(512, HD)
            s = lax.dot_general(qs[a], keys, (((1,), (1,)), ((), ())), preferred_element_type=f32)
            parts = []
            for i in range(4):
                ok = vert_ref[me * 4 + a, first + i] <= t - band_ref[me * 4 + a]
                parts.append(s[:, rows[i]] + jnp.where(ok, 0.0, NEG))
            put_scores(cc, a, parts)

    def row_top(n, a):
        m = mx[0, rows[a], :]
        for cc in range(1, n):
            m = jnp.maximum(m, mx[cc, rows[a], :])
        return jnp.max(m, axis=1, keepdims=True) * SCALE

    def weights(cc, a, top):
        return jnp.concatenate(
            [jnp.exp2(sb[cc, rows[a], rows[i]] * SCALE - top).astype(bf) for i in range(4)], axis=1
        )

    def far_sums(cc, first, a, top):
        vals = jnp.concatenate([far[pl.ds(first, 4), a, 1].reshape(512, HD), ones], axis=1)
        return jnp.dot(weights(cc, a, top), vals, preferred_element_type=f32)

    def send_out(mi):
        @pl.when(mi == my_tile)
        def _():
            orecv[pl.ds(me * 4, 4)] = ob[mi]

        @pl.when(mi != my_tile)
        def _():
            send(ob.at[mi], orecv.at[pl.ds(me * 4, 4)], o_ss.at[mi], o_rs.at[me], holder(mi)).start()

    def place(mi):
        gl = mi // 2
        j = 2 * z + mi % 2
        return (ylo * 8 + gl) * 16 + j, gl * 16 + j + 1

    def queries_of(mi):
        return [qb[mi, :, rows[a]] for a in range(4)]

    def attend_lower_groups(pos, carry):
        dx, u = (1 + 2 * (pos % 4)) % 5, pos // 4
        dc, dy = ((u + 1) // 2) % 2, 1 - u // 2
        mi = (((x + dx) % 4) * 2 + (c + dc) % 2) * 2 + (yhi + dy) % 2
        t, _ = place(mi)
        qs = queries_of(mi)
        for ch in range(2):
            far_scores(ch, 4 * ch, t, qs)

        @pl.when(mi >= 0)
        def _():
            for a in range(4):
                old = top1[mi, rows[a], :]
                top = jnp.maximum(row_top(2, a), old)
                keep = jnp.exp2(old - top)
                pv = far_sums(0, 0, a, top) + far_sums(1, 4, a, top)
                num = acc1[mi, rows[a], :] * keep + pv[:, :HD]
                mass = den1[mi, rows[a], :] * keep + pv[:, HD:]
                ob[mi, a] = (num / mass).astype(bf)

        send_out(mi)
        return carry

    def start_tail():
        tail.wait_recv()
        begin(4)

    def attend(it, carry):
        mi = (((it + 2) // 2) % 8) * 2 + (it + yhi) % 2
        for at, (n, h) in enumerate(((1, 4), (2, 3), (3, 2), (2, 4), (3, 3), (3, 4))):
            pl.when(it == at)(functools.partial(hop, n, h))
        pl.when(extra & (it == 5))(start_tail)
        for h in range(1, 5):
            pl.when(extra & (it == 5 + h))(functools.partial(hop, 4, h))

        @pl.when((it == 0) | (it == 2) | (it == 5) | (it == 7))
        def _():
            n = (3 * it + 1) // 7
            every(n, lambda q, m, zz: handed(q, m, zz).wait_recv())
            pick(n)

            @pl.when(lower)
            def _():
                to_upper(n).start()

        @pl.when(upper & ((it == 4) | (it == 6) | (it == 9) | (it == 11)))
        def _():
            n = (3 * it - 11) // 7
            to_upper(n).wait_recv()
            share(n, PLUS, z % 2).start()
            share(n, MINUS, z % 2).start()

        pl.when(upper & (c == 0) & (it == 14))(
            functools.partial(every, 4, lambda q, n, zz: handed(q, n, zz).wait_recv())
        )

        @pl.when(mi != my_tile)
        def _():
            send(q_ref.at[:, pl.ds(0, 512)], qb.at[mi], q_ss.at[1], q_rs.at[mi], twin).wait_recv()

        t, start = place(mi)
        qs = queries_of(mi)
        q4 = jnp.concatenate(qs, axis=0)
        lims = [jnp.minimum(band_ref[me * 4 + a], t + 1) for a in range(4)]
        for cc in range(4):
            keys = kv[pl.ds(start + 4 * cc, 4), 0].reshape(512, HD)
            s = lax.dot_general(q4, keys, (((1,), (1,)), ((), ())), preferred_element_type=f32)
            for a in range(4):
                parts = []
                for i in range(4):
                    off = 15 - (4 * cc + i)
                    part = s[rows[a], rows[i]]
                    if off == 0:
                        part = jnp.where(rows_id >= cols_id, part, NEG)
                    else:
                        part = part + jnp.where(off < lims[a], 0.0, NEG)
                    parts.append(part)
                put_scores(cc, a, parts)
        for ch in range(2):
            far_scores(4 + ch, ylo * 8 + 4 * ch, t, qs)

        @pl.when(mi >= 0)
        def _():
            tops = [row_top(6, a) for a in range(4)]
            acc = [None] * 4
            for cc in range(4):
                vals = jnp.concatenate([kv[pl.ds(start + 4 * cc, 4), 1].reshape(512, HD), ones], axis=1)
                p = jnp.concatenate([weights(cc, a, tops[a]) for a in range(4)], axis=0)
                pv = jnp.dot(p, vals, preferred_element_type=f32)
                for a in range(4):
                    acc[a] = pv[rows[a]] if cc == 0 else acc[a] + pv[rows[a]]
            for ch in range(2):
                for a in range(4):
                    acc[a] = acc[a] + far_sums(4 + ch, ylo * 8 + 4 * ch, a, tops[a])
            for a in range(4):
                acc1[mi, rows[a], :] = acc[a][:, :HD]
                den1[mi, rows[a], :] = acc[a][:, HD:]
                top1[mi, rows[a], :] = jnp.broadcast_to(tops[a], (TILE, HD))

        @pl.when(lower)
        def _():
            for a in range(4):
                ob[mi, a] = (acc1[mi, rows[a], :] / den1[mi, rows[a], :]).astype(bf)
            send_out(mi)

        return carry

    lax.fori_loop(0, 16, attend, 0)

    @pl.when(upper)
    def _():
        for n in range(4):
            for d in (PLUS, MINUS):
                share(n, d, 1 - z % 2).wait_recv()
        lax.fori_loop(0, 16, attend_lower_groups, 0)


    for r in range(1, 16):
        o = (me + r) % 16
        send(ob.at[0], orecv.at[pl.ds(o * 4, 4)], o_ss.at[tile_of(o)], o_rs.at[o], member(o)).wait_recv()

    for p in range(HEADS):
        out_ref[:, p * HD : (p + 1) * HD] = orecv[order_ref[p]]

    for r in range(7):
        send(kvs.at[0], kv.at[here], a_ss.at[r], a_rs.at[0], twin).wait_send()
    for r in range(1, 16):
        o = (me + r) % 16
        q_send(r).wait_send()
        send(ob.at[0], orecv.at[pl.ds(me * 4, 4)], o_ss.at[tile_of(o)], o_rs.at[me], twin).wait_send()

    @pl.when(lower & (c == 1))
    def _():
        tail.wait_send()

    def sent(n):
        every(n, lambda q, m, zz: hand(q, m, zz).wait_send())
        for d, h in ARRIVALS:
            pl.when(goes(d, h, n))(lambda d=d, h=h: ring(d, h, n).wait_send())

    def sent_in_loop(n, carry):
        sent(n)

        @pl.when(lower)
        def _():
            to_upper(n).wait_send()

        @pl.when(upper)
        def _():
            share(n, PLUS, z % 2).wait_send()
            share(n, MINUS, z % 2).wait_send()

        return carry

    lax.fori_loop(0, 4, sent_in_loop, 0)
    pl.when(extra)(functools.partial(sent, 4))


def body(queries, keys, values, band_tiles, vertical_tiles, head_order):
    dma = pltpu.SemaphoreType.DMA
    vm = pl.BlockSpec(memory_space=pltpu.VMEM)
    sm = pl.BlockSpec(memory_space=pltpu.SMEM)
    bf, f32 = jnp.bfloat16, jnp.float32
    return pl.pallas_call(
        kernel,
        out_shape=jax.ShapeDtypeStruct((TILE, HEADS * HD), bf),
        in_specs=[sm, sm, sm, vm, vm, vm],
        out_specs=vm,
        scratch_shapes=[
            pltpu.VMEM((8, 2, TILE, HD), bf),
            pltpu.VMEM((144, 2, TILE, HD), bf),
            pltpu.VMEM((16, TILE, 512), bf),
            pltpu.VMEM((16, 4, 2, TILE, HD), bf),
            pltpu.VMEM((16, 4, TILE, HD), bf),
            pltpu.VMEM((HEADS, TILE, HD), bf),
            pltpu.VMEM((6, 512, 512), f32),
            pltpu.VMEM((6, 512, HD), f32),
            pltpu.VMEM((16, 512, HD), f32),
            pltpu.VMEM((16, 512, HD), f32),
            pltpu.VMEM((16, 512, HD), f32),
            dma((16,)),
            dma((16,)),
            dma((8,)),
            dma((8,)),
            dma((2, 4, 5)),
            dma((2, 4, 5)),
            dma((9, 5)),
            dma((9, 5)),
            dma((4,)),
            dma((4,)),
            dma((4, 2)),
            dma((4, 2)),
            dma((16,)),
            dma((16,)),
            dma((2,)),
        ],
        compiler_params=pltpu.CompilerParams(
            collective_id=0, has_side_effects=True, vmem_limit_bytes=60 * 2**20
        ),
        name="attention",
    )(band_tiles, vertical_tiles, head_order, queries, keys, values)


def solution(mesh):
    tokens = P(("seq", "head"), None)
    return jax.shard_map(
        body,
        mesh=mesh,
        in_specs=(tokens, tokens, tokens, P(), P(), P()),
        out_specs=tokens,
        check_vma=False,
    )
```

```python
import functools

import jax
import jax.numpy as jnp
from jax import lax
from jax.experimental import pallas as pl
from jax.experimental.pallas import tpu as pltpu
from jax.sharding import PartitionSpec as P

HEADS = 64
HD = 128
TILE = 128
MESH = pl.DeviceIdType.MESH
NEG = -1e30
SCALE = 1.4426950408889634 * HD**-0.5
PLUS, MINUS = 0, 1
ARRIVALS = [(d, h) for h in range(1, 5) for d in (PLUS, MINUS)]

CHIPS = [(1, 0), (3, 0), (0, 1), (2, 0), (1, 1), (3, 1), (2, 1)]
PEERS = [(dx, dy, dc) for dy, dc in ((1, 0), (1, 1), (0, 1), (0, 0)) for dx in (1, 3, 0, 2)]
PEERS.remove((0, 0, 0))


def device_id(ylo, x, yhi, z, c):
    return (ylo * 8 + x * 2 + c, z * 2 + yhi)


def kernel(
    band_ref,
    vert_ref,
    order_ref,
    q_ref,
    k_ref,
    v_ref,
    out_ref,
    kvs,
    kv,
    qb,
    far,
    ob,
    orecv,
    sb,
    mx,
    acc1,
    den1,
    top1,
    q_ss,
    q_rs,
    a_ss,
    a_rs,
    z_ss,
    z_rs,
    b_ss,
    b_rs,
    y_ss,
    y_rs,
    f_ss,
    f_rs,
    o_ss,
    o_rs,
    t_s,
):
    seq, jj = lax.axis_index("seq"), lax.axis_index("head")
    ylo, x, c = seq // 8, (seq // 2) % 4, seq % 2
    z, yhi = jj // 2, jj % 2
    me = (x * 2 + yhi) * 2 + c
    kvh = x * 2 + yhi
    my_tile = (x * 2 + c) * 2 + yhi
    lower, upper = ylo == 0, ylo == 1
    extra = upper & (c == 1)
    f32, bf = jnp.float32, jnp.bfloat16
    rows = [slice(a * TILE, (a + 1) * TILE) for a in range(4)]

    def member(o):
        return device_id(ylo, o // 4, (o // 2) % 2, z, o % 2)

    def tile_of(o):
        return ((o // 4) * 2 + o % 2) * 2 + (o // 2) % 2

    def holder(mi):
        return device_id(ylo, mi // 4, mi % 2, z, (mi // 2) % 2)

    up = device_id(ylo, x, yhi, (z + 1) % 8, c)
    down = device_id(ylo, x, yhi, (z + 7) % 8, c)
    twin = device_id(ylo, x, yhi, z, 1 - c)
    across = device_id(1 - ylo, x, yhi, z, c)
    way = (up, down)

    def send(src, dst, ss, rs, dev):
        return pltpu.make_async_remote_copy(
            src_ref=src, dst_ref=dst, send_sem=ss, recv_sem=rs, device_id=dev, device_id_type=MESH
        )

    barrier = pltpu.get_barrier_semaphore()
    for r in range(1, 16):
        pl.semaphore_signal(barrier, inc=1, device_id=member((me + r) % 16), device_id_type=MESH)
    for dev in (up, down, across):
        pl.semaphore_signal(barrier, inc=1, device_id=dev, device_id_type=MESH)

    for g in range(8):
        kvs[g, 0] = k_ref[:, g * HD : (g + 1) * HD]
        kvs[g, 1] = v_ref[:, g * HD : (g + 1) * HD]

    @pl.when(lower)
    def _():
        kv[0:16] = jnp.zeros((16, 2, TILE, HD), bf)

    far[pl.ds(ylo * 8, 8)] = jnp.zeros((8, 4, 2, TILE, HD), bf)
    pl.semaphore_wait(barrier, 18)

    here = 16 + (x * 2 + c) * 16 + jj
    for r, (dx, dy) in enumerate(CHIPS):
        g = ((x + dx) % 4) * 2 + (yhi + dy) % 2
        send(kvs.at[g], kv.at[here], a_ss.at[r], a_rs.at[kvh], member(g * 2 + c)).start()
    kv[here] = kvs[kvh]

    def q_send(r):
        dx, dy, dc = PEERS[r - 1]
        o = (((x + dx) % 4) * 2 + (yhi + dy) % 2) * 2 + (c + dc) % 2
        return send(
            q_ref.at[:, pl.ds(pl.multiple_of(o * 512, 512), 512)],
            qb.at[my_tile],
            q_ss.at[r],
            q_rs.at[my_tile],
            member(o),
        )

    qb[my_tile] = q_ref[:, pl.ds(pl.multiple_of(me * 512, 512), 512)]

    def kv_landed(n):
        for yh in range(2):
            g = n * 2 + yh

            @pl.when(kvh != g)
            def _():
                at = 16 + (n * 2 + c) * 16 + 2 * z + yh
                send(kvs.at[0], kv.at[at], a_ss.at[1], a_rs.at[g], twin).wait_recv()

    def first_of(n, core, zz):
        return jnp.where(n == 4, 2 * zz, 16 + (n * 2 + core) * 16 + 2 * zz)

    def block(n, zz):
        return kv.at[pl.ds(first_of(n, c, zz), 2)]

    def origin(d, h):
        return (z + 8 - h) % 8 if d == PLUS else (z + h) % 8

    def goes(d, h, n):
        last = (n < 2) | (n == 4)
        return (h < 4) | (last if d == PLUS else jnp.logical_not(last))

    def ring(d, h, n):
        blk = block(n, origin(d, h - 1))
        return send(blk, blk, z_ss.at[d, h - 1, n], z_rs.at[d, h - 1, n], way[d])

    def ring_landing(d, h, n):
        blk = block(n, origin(d, h))
        return send(blk, blk, z_ss.at[d, h - 1, n], z_rs.at[d, h - 1, n], way[d])

    def slot(d, h):
        return 1 + (h - 1) * 2 + d

    def hand(q, n, zz):
        blk = block(n, zz)
        return send(blk, blk, b_ss.at[q, n], b_rs.at[q, n], twin)

    def handed(q, n, zz):
        blk = kv.at[pl.ds(first_of(n, 1 - c, zz), 2)]
        return send(blk, blk, b_ss.at[q, n], b_rs.at[q, n], twin)

    def begin(n):
        ring(PLUS, 1, n).start()
        ring(MINUS, 1, n).start()
        hand(0, n, z).start()

    def hop(n, h):
        for d in (PLUS, MINUS):

            @pl.when(goes(d, h, n))
            def _():
                ring_landing(d, h, n).wait_recv()

                @pl.when((h < 4) & goes(d, h + 1, n))
                def _():
                    ring(d, jnp.minimum(h + 1, 4), n).start()

                hand(slot(d, h), n, origin(d, h)).start()

    def every(n, act):
        act(0, n, z)
        for d, h in ARRIVALS:
            pl.when(goes(d, h, n))(functools.partial(act, slot(d, h), n, origin(d, h)))

    tail_src = kv.at[pl.ds(128 + 2 * z, 2)]
    tail_dst = kv.at[pl.ds(2 * z, 2)]
    tail = send(tail_src, tail_dst, t_s.at[0], t_s.at[1], across)

    kv_landed(0)
    begin(0)
    for r in range(1, 16):
        q_send(r).start()
    kv_landed(1)
    begin(1)
    hop(0, 1)
    kv_landed(2)
    begin(2)
    hop(0, 2)
    hop(1, 1)
    kv_landed(3)
    begin(3)

    @pl.when(lower & (c == 1))
    def _():
        tail.start()

    hop(0, 3)
    hop(1, 2)
    hop(2, 1)
    hop(0, 4)
    hop(1, 3)
    hop(2, 2)
    hop(3, 1)

    def pick(n):
        def one(e, carry):
            g, a = 2 * n + e // 4, e % 4
            want = vert_ref[me * 4 + a, ylo * 8 + g] & 15
            got = kv[16 + g * 16]
            for r in range(1, 16):
                got = jnp.where(want == r, kv[16 + g * 16 + r], got)
            far[ylo * 8 + g, a] = got
            return carry

        lax.fori_loop(0, 8, one, 0)

    def to_upper(n):
        blk = far.at[2 * n + z % 2]
        return send(blk, blk, y_ss.at[n], y_rs.at[n], across)

    def share(n, d, odd):
        blk = far.at[2 * n + odd, pl.ds(2 * d, 2)]
        return send(blk, blk, f_ss.at[n, d], f_rs.at[n, d], way[d])

    rows_id = lax.broadcasted_iota(jnp.int32, (TILE, TILE), 0)
    cols_id = lax.broadcasted_iota(jnp.int32, (TILE, TILE), 1)
    ones = jnp.ones((512, HD), bf)

    def put_scores(cc, a, parts):
        m = None
        for i in range(4):
            sb[cc, rows[a], rows[i]] = parts[i]
            m = parts[i] if m is None else jnp.maximum(m, parts[i])
        mx[cc, rows[a], :] = m

    def far_scores(cc, first, t, qs):
        for a in range(4):
            keys = far[pl.ds(first, 4), a, 0].reshape(512, HD)
            s = lax.dot_general(qs[a], keys, (((1,), (1,)), ((), ())), preferred_element_type=f32)
            parts = []
            for i in range(4):
                ok = vert_ref[me * 4 + a, first + i] <= t - band_ref[me * 4 + a]
                parts.append(s[:, rows[i]] + jnp.where(ok, 0.0, NEG))
            put_scores(cc, a, parts)

    def row_top(n, a):
        m = mx[0, rows[a], :]
        for cc in range(1, n):
            m = jnp.maximum(m, mx[cc, rows[a], :])
        return jnp.max(m, axis=1, keepdims=True) * SCALE

    def weights(cc, a, top):
        return jnp.concatenate(
            [jnp.exp2(sb[cc, rows[a], rows[i]] * SCALE - top).astype(bf) for i in range(4)], axis=1
        )

    def far_sums(cc, first, a, top):
        vals = jnp.concatenate([far[pl.ds(first, 4), a, 1].reshape(512, HD), ones], axis=1)
        return jnp.dot(weights(cc, a, top), vals, preferred_element_type=f32)

    def send_out(mi):
        @pl.when(mi == my_tile)
        def _():
            orecv[pl.ds(me * 4, 4)] = ob[mi]

        @pl.when(mi != my_tile)
        def _():
            send(ob.at[mi], orecv.at[pl.ds(me * 4, 4)], o_ss.at[mi], o_rs.at[me], holder(mi)).start()

    def place(mi):
        gl = mi // 2
        j = 2 * z + mi % 2
        return (ylo * 8 + gl) * 16 + j, gl * 16 + j + 1

    def queries_of(mi):
        return [qb[mi, :, rows[a]] for a in range(4)]

    def turn(pos):
        u, col = pos // 4, (x + (1 + 2 * (pos % 4)) % 5) % 4
        core = (u // 2 + (4 - col) // 4) % 2
        dy = (u + ((col + 1) // 2) % 2) % 2
        return col * 4 + core * 2 + (yhi + dy) % 2

    def send_turn(pos, carry):
        send_out(turn(pos))
        return carry

    def attend_lower_groups(pos, carry):
        mi = turn(pos)
        t, _ = place(mi)
        qs = queries_of(mi)
        for ch in range(2):
            far_scores(ch, 4 * ch, t, qs)

        @pl.when(mi >= 0)
        def _():
            for a in range(4):
                old = top1[mi, rows[a], :]
                top = jnp.maximum(row_top(2, a), old)
                keep = jnp.exp2(old - top)
                pv = far_sums(0, 0, a, top) + far_sums(1, 4, a, top)
                num = acc1[mi, rows[a], :] * keep + pv[:, :HD]
                mass = den1[mi, rows[a], :] * keep + pv[:, HD:]
                ob[mi, a] = (num / mass).astype(bf)

        send_out(mi)
        return carry

    def start_tail():
        tail.wait_recv()
        begin(4)

    def attend(it, carry):
        mi = (((it + 2) // 2) % 8) * 2 + (it + yhi) % 2
        for at, (n, h) in enumerate(((1, 4), (2, 3), (3, 2), (2, 4), (3, 3), (3, 4))):
            pl.when(it == at)(functools.partial(hop, n, h))
        pl.when(extra & (it == 5))(start_tail)
        for h in range(1, 5):
            pl.when(extra & (it == 5 + h))(functools.partial(hop, 4, h))

        @pl.when((it == 0) | (it == 2) | (it == 5) | (it == 7))
        def _():
            n = (3 * it + 1) // 7
            every(n, lambda q, m, zz: handed(q, m, zz).wait_recv())
            pick(n)

            @pl.when(lower)
            def _():
                to_upper(n).start()

        @pl.when(upper & ((it == 4) | (it == 6) | (it == 9) | (it == 11)))
        def _():
            n = (3 * it - 11) // 7
            to_upper(n).wait_recv()
            share(n, PLUS, z % 2).start()
            share(n, MINUS, z % 2).start()

        pl.when(upper & (c == 0) & (it == 14))(
            functools.partial(every, 4, lambda q, n, zz: handed(q, n, zz).wait_recv())
        )

        @pl.when(mi != my_tile)
        def _():
            send(q_ref.at[:, pl.ds(0, 512)], qb.at[mi], q_ss.at[1], q_rs.at[mi], twin).wait_recv()

        t, start = place(mi)
        qs = queries_of(mi)
        q4 = jnp.concatenate(qs, axis=0)
        lims = [jnp.minimum(band_ref[me * 4 + a], t + 1) for a in range(4)]
        for cc in range(4):
            keys = kv[pl.ds(start + 4 * cc, 4), 0].reshape(512, HD)
            s = lax.dot_general(q4, keys, (((1,), (1,)), ((), ())), preferred_element_type=f32)
            for a in range(4):
                parts = []
                for i in range(4):
                    off = 15 - (4 * cc + i)
                    part = s[rows[a], rows[i]]
                    if off == 0:
                        part = jnp.where(rows_id >= cols_id, part, NEG)
                    else:
                        part = part + jnp.where(off < lims[a], 0.0, NEG)
                    parts.append(part)
                put_scores(cc, a, parts)
        for ch in range(2):
            far_scores(4 + ch, ylo * 8 + 4 * ch, t, qs)

        @pl.when(mi >= 0)
        def _():
            tops = [row_top(6, a) for a in range(4)]
            acc = [None] * 4
            for cc in range(4):
                vals = jnp.concatenate([kv[pl.ds(start + 4 * cc, 4), 1].reshape(512, HD), ones], axis=1)
                p = jnp.concatenate([weights(cc, a, tops[a]) for a in range(4)], axis=0)
                pv = jnp.dot(p, vals, preferred_element_type=f32)
                for a in range(4):
                    acc[a] = pv[rows[a]] if cc == 0 else acc[a] + pv[rows[a]]
            for ch in range(2):
                for a in range(4):
                    acc[a] = acc[a] + far_sums(4 + ch, ylo * 8 + 4 * ch, a, tops[a])
            for a in range(4):
                acc1[mi, rows[a], :] = acc[a][:, :HD]
                den1[mi, rows[a], :] = acc[a][:, HD:]
                top1[mi, rows[a], :] = jnp.broadcast_to(tops[a], (TILE, HD))

        @pl.when(lower)
        def _():
            for a in range(4):
                ob[mi, a] = (acc1[mi, rows[a], :] / den1[mi, rows[a], :]).astype(bf)

        @pl.when(lower & (it >= 12))
        def _():
            lax.fori_loop(4 * (it - 12), 4 * (it - 11), send_turn, 0)

        @pl.when(upper & (it == 12))
        def _():
            for n in range(4):
                for d in (PLUS, MINUS):
                    share(n, d, 1 - z % 2).wait_recv()

        @pl.when(upper & (it >= 12))
        def _():
            lax.fori_loop(4 * (it - 12), 4 * (it - 11), attend_lower_groups, 0)

        return carry

    lax.fori_loop(0, 16, attend, 0)

    for r in range(1, 16):
        o = (me + r) % 16
        send(ob.at[0], orecv.at[pl.ds(o * 4, 4)], o_ss.at[tile_of(o)], o_rs.at[o], member(o)).wait_recv()

    for p in range(HEADS):
        out_ref[:, p * HD : (p + 1) * HD] = orecv[order_ref[p]]

    for r in range(7):
        send(kvs.at[0], kv.at[here], a_ss.at[r], a_rs.at[0], twin).wait_send()
    for r in range(1, 16):
        o = (me + r) % 16
        q_send(r).wait_send()
        send(ob.at[0], orecv.at[pl.ds(me * 4, 4)], o_ss.at[tile_of(o)], o_rs.at[me], twin).wait_send()

    @pl.when(lower & (c == 1))
    def _():
        tail.wait_send()

    def sent(n):
        every(n, lambda q, m, zz: hand(q, m, zz).wait_send())
        for d, h in ARRIVALS:
            pl.when(goes(d, h, n))(lambda d=d, h=h: ring(d, h, n).wait_send())

    def sent_in_loop(n, carry):
        sent(n)

        @pl.when(lower)
        def _():
            to_upper(n).wait_send()

        @pl.when(upper)
        def _():
            share(n, PLUS, z % 2).wait_send()
            share(n, MINUS, z % 2).wait_send()

        return carry

    lax.fori_loop(0, 4, sent_in_loop, 0)
    pl.when(extra)(functools.partial(sent, 4))


def body(queries, keys, values, band_tiles, vertical_tiles, head_order):
    dma = pltpu.SemaphoreType.DMA
    vm = pl.BlockSpec(memory_space=pltpu.VMEM)
    sm = pl.BlockSpec(memory_space=pltpu.SMEM)
    bf, f32 = jnp.bfloat16, jnp.float32
    return pl.pallas_call(
        kernel,
        out_shape=jax.ShapeDtypeStruct((TILE, HEADS * HD), bf),
        in_specs=[sm, sm, sm, vm, vm, vm],
        out_specs=vm,
        scratch_shapes=[
            pltpu.VMEM((8, 2, TILE, HD), bf),
            pltpu.VMEM((144, 2, TILE, HD), bf),
            pltpu.VMEM((16, TILE, 512), bf),
            pltpu.VMEM((16, 4, 2, TILE, HD), bf),
            pltpu.VMEM((16, 4, TILE, HD), bf),
            pltpu.VMEM((HEADS, TILE, HD), bf),
            pltpu.VMEM((6, 512, 512), f32),
            pltpu.VMEM((6, 512, HD), f32),
            pltpu.VMEM((16, 512, HD), f32),
            pltpu.VMEM((16, 512, HD), f32),
            pltpu.VMEM((16, 512, HD), f32),
            dma((16,)),
            dma((16,)),
            dma((8,)),
            dma((8,)),
            dma((2, 4, 5)),
            dma((2, 4, 5)),
            dma((9, 5)),
            dma((9, 5)),
            dma((4,)),
            dma((4,)),
            dma((4, 2)),
            dma((4, 2)),
            dma((16,)),
            dma((16,)),
            dma((2,)),
        ],
        compiler_params=pltpu.CompilerParams(
            collective_id=0, has_side_effects=True, vmem_limit_bytes=60 * 2**20
        ),
        name="attention",
    )(band_tiles, vertical_tiles, head_order, queries, keys, values)


def solution(mesh):
    tokens = P(("seq", "head"), None)
    return jax.shard_map(
        body,
        mesh=mesh,
        in_specs=(tokens, tokens, tokens, P(), P(), P()),
        out_specs=tokens,
        check_vma=False,
    )
```

```python
import functools

import jax
import jax.numpy as jnp
from jax import lax
from jax.experimental import pallas as pl
from jax.experimental.pallas import tpu as pltpu
from jax.sharding import PartitionSpec as P

HEADS = 64
HD = 128
TILE = 128
MESH = pl.DeviceIdType.MESH
NEG = -1e30
SCALE = 1.4426950408889634 * HD**-0.5
PLUS, MINUS = 0, 1
ARRIVALS = [(d, h) for h in range(1, 5) for d in (PLUS, MINUS)]

CHIPS = [(1, 0), (3, 0), (0, 1), (2, 0), (1, 1), (3, 1), (2, 1)]
PEERS = [(dx, dy, dc) for dy, dc in ((1, 0), (1, 1), (0, 1), (0, 0)) for dx in (1, 3, 0, 2)]
PEERS.remove((0, 0, 0))


def device_id(ylo, x, yhi, z, c):
    return (ylo * 8 + x * 2 + c, z * 2 + yhi)


def kernel(
    band_ref,
    vert_ref,
    order_ref,
    q_ref,
    k_ref,
    v_ref,
    out_ref,
    kvs,
    kv,
    qb,
    far,
    ob,
    orecv,
    sb,
    mx,
    acc1,
    den1,
    top1,
    q_ss,
    q_rs,
    a_ss,
    a_rs,
    z_ss,
    z_rs,
    b_ss,
    b_rs,
    y_ss,
    y_rs,
    f_ss,
    f_rs,
    o_ss,
    o_rs,
    t_s,
):
    seq, jj = lax.axis_index("seq"), lax.axis_index("head")
    ylo, x, c = seq // 8, (seq // 2) % 4, seq % 2
    z, yhi = jj // 2, jj % 2
    me = (x * 2 + yhi) * 2 + c
    kvh = x * 2 + yhi
    my_tile = (x * 2 + c) * 2 + yhi
    lower, upper = ylo == 0, ylo == 1
    extra = upper & (c == 1)
    f32, bf = jnp.float32, jnp.bfloat16
    rows = [slice(a * TILE, (a + 1) * TILE) for a in range(4)]

    def member(o):
        return device_id(ylo, o // 4, (o // 2) % 2, z, o % 2)

    def tile_of(o):
        return ((o // 4) * 2 + o % 2) * 2 + (o // 2) % 2

    def holder(mi):
        return device_id(ylo, mi // 4, mi % 2, z, (mi // 2) % 2)

    up = device_id(ylo, x, yhi, (z + 1) % 8, c)
    down = device_id(ylo, x, yhi, (z + 7) % 8, c)
    twin = device_id(ylo, x, yhi, z, 1 - c)
    across = device_id(1 - ylo, x, yhi, z, c)
    way = (up, down)

    def send(src, dst, ss, rs, dev):
        return pltpu.make_async_remote_copy(
            src_ref=src, dst_ref=dst, send_sem=ss, recv_sem=rs, device_id=dev, device_id_type=MESH
        )

    barrier = pltpu.get_barrier_semaphore()
    for r in range(1, 16):
        pl.semaphore_signal(barrier, inc=1, device_id=member((me + r) % 16), device_id_type=MESH)
    for dev in (up, down, across):
        pl.semaphore_signal(barrier, inc=1, device_id=dev, device_id_type=MESH)

    for g in range(8):
        kvs[g, 0] = k_ref[:, g * HD : (g + 1) * HD]
        kvs[g, 1] = v_ref[:, g * HD : (g + 1) * HD]

    @pl.when(lower)
    def _():
        kv[0:16] = jnp.zeros((16, 2, TILE, HD), bf)

    far[pl.ds(ylo * 8, 8)] = jnp.zeros((8, 4, 2, TILE, HD), bf)
    pl.semaphore_wait(barrier, 18)

    here = 16 + (x * 2 + c) * 16 + jj
    for r, (dx, dy) in enumerate(CHIPS):
        g = ((x + dx) % 4) * 2 + (yhi + dy) % 2
        send(kvs.at[g], kv.at[here], a_ss.at[r], a_rs.at[kvh], member(g * 2 + c)).start()
    kv[here] = kvs[kvh]

    def q_send(r):
        dx, dy, dc = PEERS[r - 1]
        o = (((x + dx) % 4) * 2 + (yhi + dy) % 2) * 2 + (c + dc) % 2
        return send(
            q_ref.at[:, pl.ds(pl.multiple_of(o * 512, 512), 512)],
            qb.at[my_tile],
            q_ss.at[r],
            q_rs.at[my_tile],
            member(o),
        )

    qb[my_tile] = q_ref[:, pl.ds(pl.multiple_of(me * 512, 512), 512)]

    def kv_landed(n):
        for yh in range(2):
            g = n * 2 + yh

            @pl.when(kvh != g)
            def _():
                at = 16 + (n * 2 + c) * 16 + 2 * z + yh
                send(kvs.at[0], kv.at[at], a_ss.at[1], a_rs.at[g], twin).wait_recv()

    def first_of(n, core, zz):
        return jnp.where(n == 4, 2 * zz, 16 + (n * 2 + core) * 16 + 2 * zz)

    def block(n, zz):
        return kv.at[pl.ds(first_of(n, c, zz), 2)]

    def origin(d, h):
        return (z + 8 - h) % 8 if d == PLUS else (z + h) % 8

    def goes(d, h, n):
        last = (n < 2) | (n == 4)
        return (h < 4) | (last if d == PLUS else jnp.logical_not(last))

    def ring(d, h, n):
        blk = block(n, origin(d, h - 1))
        return send(blk, blk, z_ss.at[d, h - 1, n], z_rs.at[d, h - 1, n], way[d])

    def ring_landing(d, h, n):
        blk = block(n, origin(d, h))
        return send(blk, blk, z_ss.at[d, h - 1, n], z_rs.at[d, h - 1, n], way[d])

    def slot(d, h):
        return 1 + (h - 1) * 2 + d

    def hand(q, n, zz):
        blk = block(n, zz)
        return send(blk, blk, b_ss.at[q, n], b_rs.at[q, n], twin)

    def handed(q, n, zz):
        blk = kv.at[pl.ds(first_of(n, 1 - c, zz), 2)]
        return send(blk, blk, b_ss.at[q, n], b_rs.at[q, n], twin)

    def begin(n):
        ring(PLUS, 1, n).start()
        ring(MINUS, 1, n).start()
        hand(0, n, z).start()

    def hop(n, h):
        for d in (PLUS, MINUS):

            @pl.when(goes(d, h, n))
            def _():
                ring_landing(d, h, n).wait_recv()

                @pl.when((h < 4) & goes(d, h + 1, n))
                def _():
                    ring(d, jnp.minimum(h + 1, 4), n).start()

                hand(slot(d, h), n, origin(d, h)).start()

    def every(n, act):
        act(0, n, z)
        for d, h in ARRIVALS:
            pl.when(goes(d, h, n))(functools.partial(act, slot(d, h), n, origin(d, h)))

    tail_src = kv.at[pl.ds(128 + 2 * z, 2)]
    tail_dst = kv.at[pl.ds(2 * z, 2)]
    tail = send(tail_src, tail_dst, t_s.at[0], t_s.at[1], across)

    kv_landed(0)
    begin(0)
    for r in range(1, 16):
        q_send(r).start()
    kv_landed(1)
    begin(1)
    hop(0, 1)
    kv_landed(2)
    begin(2)
    hop(0, 2)
    hop(1, 1)
    kv_landed(3)
    begin(3)

    @pl.when(lower & (c == 1))
    def _():
        tail.start()

    hop(0, 3)
    hop(1, 2)
    hop(2, 1)
    hop(0, 4)
    hop(1, 3)
    hop(2, 2)
    hop(3, 1)

    def pick(n):
        def one(e, carry):
            g, a = 2 * n + e // 4, e % 4
            want = vert_ref[me * 4 + a, ylo * 8 + g] & 15
            got = kv[16 + g * 16]
            for r in range(1, 16):
                got = jnp.where(want == r, kv[16 + g * 16 + r], got)
            far[ylo * 8 + g, a] = got
            return carry

        lax.fori_loop(0, 8, one, 0)

    def to_upper(n):
        blk = far.at[2 * n + z % 2]
        return send(blk, blk, y_ss.at[n], y_rs.at[n], across)

    def share(n, d, odd):
        blk = far.at[2 * n + odd, pl.ds(2 * d, 2)]
        return send(blk, blk, f_ss.at[n, d], f_rs.at[n, d], way[d])

    rows_id = lax.broadcasted_iota(jnp.int32, (TILE, TILE), 0)
    cols_id = lax.broadcasted_iota(jnp.int32, (TILE, TILE), 1)
    ones = jnp.ones((512, HD), bf)

    def put_scores(cc, a, parts):
        m = None
        for i in range(4):
            sb[cc, rows[a], rows[i]] = parts[i]
            m = parts[i] if m is None else jnp.maximum(m, parts[i])
        mx[cc, rows[a], :] = m

    def far_scores(cc, first, t, qs):
        for a in range(4):
            keys = far[pl.ds(first, 4), a, 0].reshape(512, HD)
            s = lax.dot_general(qs[a], keys, (((1,), (1,)), ((), ())), preferred_element_type=f32)
            parts = []
            for i in range(4):
                ok = vert_ref[me * 4 + a, first + i] <= t - band_ref[me * 4 + a]
                parts.append(s[:, rows[i]] + jnp.where(ok, 0.0, NEG))
            put_scores(cc, a, parts)

    def row_top(n, a):
        m = mx[0, rows[a], :]
        for cc in range(1, n):
            m = jnp.maximum(m, mx[cc, rows[a], :])
        return jnp.max(m, axis=1, keepdims=True) * SCALE

    def weights(cc, a, top):
        return jnp.concatenate(
            [jnp.exp2(sb[cc, rows[a], rows[i]] * SCALE - top).astype(bf) for i in range(4)], axis=1
        )

    def far_sums(cc, first, a, top):
        vals = jnp.concatenate([far[pl.ds(first, 4), a, 1].reshape(512, HD), ones], axis=1)
        return jnp.dot(weights(cc, a, top), vals, preferred_element_type=f32)

    def send_out(mi):
        @pl.when(mi == my_tile)
        def _():
            orecv[pl.ds(me * 4, 4)] = ob[mi]

        @pl.when(mi != my_tile)
        def _():
            send(ob.at[mi], orecv.at[pl.ds(me * 4, 4)], o_ss.at[mi], o_rs.at[me], holder(mi)).start()

    def place(mi):
        gl = mi // 2
        j = 2 * z + mi % 2
        return (ylo * 8 + gl) * 16 + j, gl * 16 + j + 1

    def queries_of(mi):
        return [qb[mi, :, rows[a]] for a in range(4)]

    def turn(pos):
        u, col = pos // 4, (x + (1 + 2 * (pos % 4)) % 5) % 4
        core = (u // 2 + (4 - col) // 4) % 2
        dy = (u + ((col + 1) // 2) % 2) % 2
        return col * 4 + core * 2 + (yhi + dy) % 2

    def send_turn(pos, carry):
        send_out(turn(pos))
        return carry

    def attend_lower_groups(pos, carry):
        mi = turn(pos)
        t, _ = place(mi)
        qs = queries_of(mi)
        for ch in range(2):
            far_scores(ch, 4 * ch, t, qs)

        @pl.when(mi >= 0)
        def _():
            for a in range(4):
                old = top1[mi, rows[a], :]
                top = jnp.maximum(row_top(2, a), old)
                keep = jnp.exp2(old - top)
                pv = far_sums(0, 0, a, top) + far_sums(1, 4, a, top)
                num = acc1[mi, rows[a], :] * keep + pv[:, :HD]
                mass = den1[mi, rows[a], :] * keep + pv[:, HD:]
                ob[mi, a] = (num / mass).astype(bf)

        send_out(mi)
        return carry

    def start_tail():
        tail.wait_recv()
        begin(4)

    def attend(it, carry):
        mi = (((it + 2) // 2) % 8) * 2 + (it + yhi) % 2
        for at, (n, h) in enumerate(((1, 4), (2, 3), (3, 2), (2, 4), (3, 3), (3, 4))):
            pl.when(it == at)(functools.partial(hop, n, h))
        pl.when(extra & (it == 5))(start_tail)
        for h in range(1, 5):
            pl.when(extra & (it == 5 + h))(functools.partial(hop, 4, h))

        @pl.when((it == 0) | (it == 2) | (it == 5) | (it == 7))
        def _():
            n = (3 * it + 1) // 7
            every(n, lambda q, m, zz: handed(q, m, zz).wait_recv())
            pick(n)

            @pl.when(lower)
            def _():
                to_upper(n).start()

        @pl.when(upper & ((it == 4) | (it == 6) | (it == 9) | (it == 11)))
        def _():
            n = (3 * it - 11) // 7
            to_upper(n).wait_recv()
            share(n, PLUS, z % 2).start()
            share(n, MINUS, z % 2).start()

        pl.when(upper & (c == 0) & (it == 14))(
            functools.partial(every, 4, lambda q, n, zz: handed(q, n, zz).wait_recv())
        )

        @pl.when(mi != my_tile)
        def _():
            send(q_ref.at[:, pl.ds(0, 512)], qb.at[mi], q_ss.at[1], q_rs.at[mi], twin).wait_recv()

        t, start = place(mi)
        qs = queries_of(mi)
        q4 = jnp.concatenate(qs, axis=0)
        lims = [jnp.minimum(band_ref[me * 4 + a], t + 1) for a in range(4)]
        for cc in range(4):
            keys = kv[pl.ds(start + 4 * cc, 4), 0].reshape(512, HD)
            s = lax.dot_general(q4, keys, (((1,), (1,)), ((), ())), preferred_element_type=f32)
            for a in range(4):
                parts = []
                for i in range(4):
                    off = 15 - (4 * cc + i)
                    part = s[rows[a], rows[i]]
                    if off == 0:
                        part = jnp.where(rows_id >= cols_id, part, NEG)
                    else:
                        part = part + jnp.where(off < lims[a], 0.0, NEG)
                    parts.append(part)
                put_scores(cc, a, parts)
        for ch in range(2):
            far_scores(4 + ch, ylo * 8 + 4 * ch, t, qs)

        @pl.when(mi >= 0)
        def _():
            tops = [row_top(6, a) for a in range(4)]
            acc = [None] * 4
            for cc in range(4):
                vals = jnp.concatenate([kv[pl.ds(start + 4 * cc, 4), 1].reshape(512, HD), ones], axis=1)
                p = jnp.concatenate([weights(cc, a, tops[a]) for a in range(4)], axis=0)
                pv = jnp.dot(p, vals, preferred_element_type=f32)
                for a in range(4):
                    acc[a] = pv[rows[a]] if cc == 0 else acc[a] + pv[rows[a]]
            for ch in range(2):
                for a in range(4):
                    acc[a] = acc[a] + far_sums(4 + ch, ylo * 8 + 4 * ch, a, tops[a])
            for a in range(4):
                acc1[mi, rows[a], :] = acc[a][:, :HD]
                den1[mi, rows[a], :] = acc[a][:, HD:]
                top1[mi, rows[a], :] = jnp.broadcast_to(tops[a], (TILE, HD))

        @pl.when(lower)
        def _():
            for a in range(4):
                ob[mi, a] = (acc1[mi, rows[a], :] / den1[mi, rows[a], :]).astype(bf)

        @pl.when(lower & (it >= 14))
        def _():
            lax.fori_loop(8 * (it - 14), 8 * (it - 13), send_turn, 0)

        @pl.when(upper & (it == 12))
        def _():
            for n in range(4):
                for d in (PLUS, MINUS):
                    share(n, d, 1 - z % 2).wait_recv()

        @pl.when(upper & (it >= 12))
        def _():
            lax.fori_loop(4 * (it - 12), 4 * (it - 11), attend_lower_groups, 0)

        return carry

    lax.fori_loop(0, 16, attend, 0)

    for r in range(1, 16):
        o = (me + r) % 16
        send(ob.at[0], orecv.at[pl.ds(o * 4, 4)], o_ss.at[tile_of(o)], o_rs.at[o], member(o)).wait_recv()

    for p in range(HEADS):
        out_ref[:, p * HD : (p + 1) * HD] = orecv[order_ref[p]]

    for r in range(7):
        send(kvs.at[0], kv.at[here], a_ss.at[r], a_rs.at[0], twin).wait_send()
    for r in range(1, 16):
        o = (me + r) % 16
        q_send(r).wait_send()
        send(ob.at[0], orecv.at[pl.ds(me * 4, 4)], o_ss.at[tile_of(o)], o_rs.at[me], twin).wait_send()

    @pl.when(lower & (c == 1))
    def _():
        tail.wait_send()

    def sent(n):
        every(n, lambda q, m, zz: hand(q, m, zz).wait_send())
        for d, h in ARRIVALS:
            pl.when(goes(d, h, n))(lambda d=d, h=h: ring(d, h, n).wait_send())

    def sent_in_loop(n, carry):
        sent(n)

        @pl.when(lower)
        def _():
            to_upper(n).wait_send()

        @pl.when(upper)
        def _():
            share(n, PLUS, z % 2).wait_send()
            share(n, MINUS, z % 2).wait_send()

        return carry

    lax.fori_loop(0, 4, sent_in_loop, 0)
    pl.when(extra)(functools.partial(sent, 4))


def body(queries, keys, values, band_tiles, vertical_tiles, head_order):
    dma = pltpu.SemaphoreType.DMA
    vm = pl.BlockSpec(memory_space=pltpu.VMEM)
    sm = pl.BlockSpec(memory_space=pltpu.SMEM)
    bf, f32 = jnp.bfloat16, jnp.float32
    return pl.pallas_call(
        kernel,
        out_shape=jax.ShapeDtypeStruct((TILE, HEADS * HD), bf),
        in_specs=[sm, sm, sm, vm, vm, vm],
        out_specs=vm,
        scratch_shapes=[
            pltpu.VMEM((8, 2, TILE, HD), bf),
            pltpu.VMEM((144, 2, TILE, HD), bf),
            pltpu.VMEM((16, TILE, 512), bf),
            pltpu.VMEM((16, 4, 2, TILE, HD), bf),
            pltpu.VMEM((16, 4, TILE, HD), bf),
            pltpu.VMEM((HEADS, TILE, HD), bf),
            pltpu.VMEM((6, 512, 512), f32),
            pltpu.VMEM((6, 512, HD), f32),
            pltpu.VMEM((16, 512, HD), f32),
            pltpu.VMEM((16, 512, HD), f32),
            pltpu.VMEM((16, 512, HD), f32),
            dma((16,)),
            dma((16,)),
            dma((8,)),
            dma((8,)),
            dma((2, 4, 5)),
            dma((2, 4, 5)),
            dma((9, 5)),
            dma((9, 5)),
            dma((4,)),
            dma((4,)),
            dma((4, 2)),
            dma((4, 2)),
            dma((16,)),
            dma((16,)),
            dma((2,)),
        ],
        compiler_params=pltpu.CompilerParams(
            collective_id=0, has_side_effects=True, vmem_limit_bytes=60 * 2**20
        ),
        name="attention",
    )(band_tiles, vertical_tiles, head_order, queries, keys, values)


def solution(mesh):
    tokens = P(("seq", "head"), None)
    return jax.shard_map(
        body,
        mesh=mesh,
        in_specs=(tokens, tokens, tokens, P(), P(), P()),
        out_specs=tokens,
        check_vma=False,
    )
```
